128 devices in a mesh: gx: 8 (over y, core), gy: 16 (over z, x).
Axes of the slice: x: 4, y: 4, z: 4, core: 2. Of those that a mesh axis runs over, the one named last changes fastest.
Arguments:
- nest_fields: bfloat16 [5, 16, 2048, 2048], P(None, None, 'gy', 'gx'), may hold values from -4 to 4, as said below
- parent_modes: float32 [5, 16, 64, 64], replicated, may hold values from -0.2 to 0.2
- nest_offset: int32 [2], replicated, may hold values from 0 to 2047
- level_mask: int32 [16], replicated, may hold values 0 or 1
- strength: float32 [5], replicated, may hold values from 0.2 to 1
Outputs:
- nudged: bfloat16 [5, 16, 2048, 2048], P(None, None, 'gy', 'gx')
The draws below stay inside these ranges and needn't reach their ends.
Inputs may be any that keep to these rules, and one draw needn't show every extreme that they name: `nest_fields`: nest fields hold large-scale waves of every field and level beside small-scale noise.
All inputs are finite; a program needn't handle non-finite values.
Results may differ from the reference program's by a relative error of at most 0.0012.
Values sent between devices are 32-bit elements; how exact they have to be, the bound alone decides.
No kernel may reach another device: no remote copies, remote signals or barrier semaphores. Data moves between devices by JAX's collectives and lax.ppermute only.
A program may use at most 64 MiB of HBM per device.

```python
import math
import jax
import jax.numpy as jnp
from jax import lax

FIELDS = 5
MODES = 64
LEVELS = 16
NX = 2048
NY = 2048


def draw_nest_fields(key, part):
    key = jax.random.fold_in(key, 11)
    wave_keys = jax.random.split(key, 8)
    amplitude_cap = 0.4
    reach = MODES // 2 + 8
    rows_pos = jnp.arange(NY, dtype=jnp.int32)
    cols_pos = jnp.arange(NX, dtype=jnp.int32)
    smooth = jnp.zeros((FIELDS, LEVELS, NY, NX), jnp.float32)
    for wave_index in range(6):
        inner_keys = jax.random.split(wave_keys[wave_index], 4)
        wave_x = jax.random.randint(inner_keys[0], (FIELDS, LEVELS), 0, reach)
        wave_y = jax.random.randint(inner_keys[1], (FIELDS, LEVELS), 0, reach)
        amplitude = jax.random.uniform(inner_keys[2], (FIELDS, LEVELS), jnp.float32, -amplitude_cap, amplitude_cap)
        start_phase = jax.random.uniform(inner_keys[3], (FIELDS, LEVELS), jnp.float32, 0.0, 1.0)
        phase_y = (wave_y[:, :, None] * rows_pos[None, None, :] % NY).astype(jnp.float32) / NY
        phase_y = 2.0 * math.pi * (phase_y + start_phase[:, :, None])
        phase_x = 2.0 * math.pi * (wave_x[:, :, None] * cols_pos[None, None, :] % NX).astype(jnp.float32) / NX
        product_cos = jnp.cos(phase_y)[:, :, :, None] * jnp.cos(phase_x)[:, :, None, :]
        product_sin = jnp.sin(phase_y)[:, :, :, None] * jnp.sin(phase_x)[:, :, None, :]
        smooth = smooth + amplitude[:, :, None, None] * (product_cos - product_sin)
    noise = jnp.clip(0.5 * jax.random.normal(wave_keys[7], (FIELDS, LEVELS, NY, NX), jnp.float32), -1.5, 1.5)
    return (smooth + noise).astype(jnp.bfloat16)


def set_ends(drawn, rng, smallest, top_value):
    spot = [jax.random.randint(jax.random.fold_in(rng, axis), (), 0, length) for axis, length in enumerate(drawn.shape)]
    longest = drawn.shape.index(max(drawn.shape))
    beside = spot[:longest] + [(spot[longest] + 1) % drawn.shape[longest]] + spot[longest + 1:]
    return drawn.at[tuple(spot)].set(smallest).at[tuple(beside)].set(top_value)


def centred(stream_key, shape, scale, bound, kind=jnp.bfloat16):
    return jnp.clip(scale * jax.random.normal(stream_key, shape, jnp.float32), -bound, bound).astype(kind)


def setup_inputs(seed: int = 0) -> dict:
    key_list = jax.random.split(jax.random.key(seed), 6)
    return {
        "nest_fields": draw_nest_fields(jax.random.fold_in(key_list[5], 71), 0),
        "parent_modes": centred(key_list[1], (FIELDS, LEVELS, MODES, MODES), 0.03, 0.2, jnp.float32),
        "nest_offset": jax.random.randint(key_list[2], (2,), 0, NX).astype(jnp.int32),
        "level_mask": set_ends((jax.random.randint(key_list[3], (LEVELS,), 0, 4) < 3).astype(jnp.int32), jax.random.fold_in(key_list[3], 1), 0, 1),
        "strength": jnp.clip(jnp.exp(jax.random.uniform(key_list[4], (FIELDS,), jnp.float32, math.log(0.2), math.log(1.0))), 0.2, 1.0),
    }


def wave_table(mode_count, full_length, cell_shift):
    positions = (jnp.arange(full_length, dtype=jnp.int32) + cell_shift) % full_length
    half_count = mode_count // 2
    wavenumbers = jnp.concatenate([jnp.arange(half_count, dtype=jnp.int32), jnp.arange(1, half_count + 1, dtype=jnp.int32)])
    phase_int = (wavenumbers[:, None] * positions[None, :]) % full_length
    angles = (2.0 * math.pi / full_length) * phase_int.astype(jnp.float32)
    is_cosine = jnp.arange(mode_count, dtype=jnp.int32)[:, None] < half_count
    return jnp.where(is_cosine, jnp.cos(angles), jnp.sin(angles))


def reference(nest_fields, parent_modes, nest_offset, level_mask, strength):
    highest = lax.Precision.HIGHEST
    zero_shift = jnp.zeros((), jnp.int32)
    table_x = wave_table(MODES, NX, zero_shift)
    table_y = wave_table(MODES, NY, zero_shift)
    shift_x = wave_table(MODES, NX, nest_offset[0].astype(jnp.int32))
    shift_y = wave_table(MODES, NY, nest_offset[1].astype(jnp.int32))
    rounded_x = table_x.astype(jnp.bfloat16).astype(jnp.float32)
    weights = jnp.where(jnp.arange(MODES) == 0, 1.0, 2.0).astype(jnp.float32)
    mode_scale = weights[:, None] * weights[None, :] / (NX * NY)
    slab_fields = nest_fields.reshape(FIELDS * LEVELS, NY, NX)
    slab_parents = parent_modes.reshape(FIELDS * LEVELS, MODES, MODES)
    blend_gain = (strength[:, None] * level_mask[None, :].astype(jnp.float32)).reshape(-1)

    def nudge_slab(packed):
        slab_field, slab_parent, slab_gain = packed
        wide_field = slab_field.astype(jnp.float32)
        along_x = jnp.dot(wide_field, rounded_x.T, precision=highest)
        nest_modes = jnp.dot(table_y, along_x, precision=highest) * mode_scale
        parent_cols = jnp.dot(slab_parent, shift_x, precision=highest)
        nest_cols = jnp.dot(nest_modes, table_x, precision=highest)
        correction = jnp.dot(shift_y.T, parent_cols, precision=highest) - jnp.dot(table_y.T, nest_cols, precision=highest)
        return (wide_field + slab_gain * correction).astype(jnp.bfloat16)

    nudged = lax.map(nudge_slab, (slab_fields, slab_parents, blend_gain))
    return nudged.reshape(FIELDS, LEVELS, NY, NX)
```

```python
import functools
import math

import jax
import jax.numpy as jnp
import numpy as np
from jax import lax
from jax.experimental import pallas as pl
from jax.experimental.pallas import tpu as pltpu
from jax.sharding import PartitionSpec as P

MODES = 64
HALF = MODES // 2
CELLS = 2048
ROWS = 128
COLS = 256
SLABS = 80
LEVELS = 16
PAIRS = SLABS // 2
HALF_PAIRS = PAIRS // 2
F32 = jnp.float32
BF16 = jnp.bfloat16
VMEM_LIMIT = 48 * 1024 * 1024


def split_bf16(value):
    high = value.astype(BF16)
    low = (value - high.astype(F32)).astype(BF16)
    return high, low


def numpy_table():
    wave = np.concatenate([np.arange(HALF), np.arange(1, HALF + 1)])
    phase = (wave[:, None] * np.arange(CELLS)[None, :]) % CELLS
    angle = phase * (2.0 * math.pi / CELLS)
    cosine = np.arange(MODES)[:, None] < HALF
    return np.where(cosine, np.cos(angle), np.sin(angle)).astype(np.float32)


def forward_constants():
    table = numpy_table()
    rounded = table.astype(BF16)
    columns = np.concatenate([rounded.T, rounded.T], axis=1)
    high = rounded
    low = (table - high.astype(np.float32)).astype(BF16)
    tiles = CELLS // ROWS
    high = high.reshape(MODES, tiles, ROWS).transpose(1, 0, 2)
    low = low.reshape(MODES, tiles, ROWS).transpose(1, 0, 2)
    rows = np.concatenate([high, high, low], axis=2)
    return columns, rows


def forward_kernel(place_ref, field_ref, cols_ref, rows_ref, out_ref, weight_ref):
    @pl.when(pl.program_id(0) == 0)
    def _():
        table = cols_ref[...]
        lane = lax.broadcasted_iota(jnp.int32, table.shape, 1)
        zero = jnp.zeros_like(table)
        weight_ref[0:COLS, :] = jnp.where(lane < MODES, table, zero)
        weight_ref[COLS:, :] = jnp.where(lane < MODES, zero, table)

    pairs = field_ref.shape[0]
    left = field_ref[:, 0].reshape(pairs * ROWS, COLS)
    right = field_ref[:, 1].reshape(pairs * ROWS, COLS)
    along = jnp.dot(left, weight_ref[0:COLS, :], preferred_element_type=F32)
    along += jnp.dot(right, weight_ref[COLS:, :], preferred_element_type=F32)
    table_y = rows_ref[0]
    for quad in range(pairs // 2):
        first = along[(2 * quad) * ROWS : (2 * quad + 1) * ROWS]
        second = along[(2 * quad + 1) * ROWS : (2 * quad + 2) * ROWS]
        high, low = split_bf16(jnp.concatenate([first, second], axis=1))
        stacked = jnp.concatenate([high, low, high], axis=0)
        sums = jnp.dot(table_y, stacked, preferred_element_type=F32)
        out_ref[2 * quad] = sums[:, 0:128]
        out_ref[2 * quad + 1] = sums[:, 128:256]


def forward(place, field, columns, rows, steps):
    block = HALF_PAIRS // steps
    return pl.pallas_call(
        forward_kernel,
        grid_spec=pltpu.PrefetchScalarGridSpec(
            num_scalar_prefetch=1,
            grid=(steps,),
            in_specs=[
                pl.BlockSpec((block, 2, ROWS, COLS), lambda i, s: (s[0] * steps + i, 0, 0, 0)),
                pl.BlockSpec((COLS, 128), lambda i, s: (s[1], 0)),
                pl.BlockSpec((1, MODES, 3 * ROWS), lambda i, s: (s[2], 0, 0)),
            ],
            out_specs=pl.BlockSpec((block, MODES, 128), lambda i, s: (i, 0, 0)),
            scratch_shapes=[pltpu.VMEM((2 * COLS, 128), BF16)],
        ),
        out_shape=jax.ShapeDtypeStruct((HALF_PAIRS, MODES, 128), F32),
        compiler_params=pltpu.CompilerParams(vmem_limit_bytes=VMEM_LIMIT),
        cost_estimate=pl.CostEstimate(
            flops=2 * HALF_PAIRS * 2 * ROWS * COLS * MODES,
            bytes_accessed=HALF_PAIRS * 2 * ROWS * COLS * 2 + HALF_PAIRS * MODES * 128 * 4,
            transcendentals=0,
        ),
        name="forward_modes",
    )(place, field, columns, rows)


def wave_sine(wave, cosine, position):
    phase = wave * position + jnp.where(cosine, CELLS // 4, 0)
    phase = ((phase + CELLS // 2) & (CELLS - 1)) - CELLS // 2
    return jnp.sin(phase.astype(F32) * (2.0 * math.pi / CELLS))


def tables_kernel(place_ref, offset_ref, rows_ref, even_ref, odd_ref):
    first_x = place_ref[1] * COLS
    first_y = place_ref[2] * ROWS
    shift_x = offset_ref[0]
    shift_y = offset_ref[1]
    mode = lax.broadcasted_iota(jnp.int32, (ROWS, 128), 1)
    position = lax.broadcasted_iota(jnp.int32, (ROWS, 128), 0) + first_y
    shifted = mode >= MODES
    mode = mode & (MODES - 1)
    wave = jnp.where(mode < HALF, mode, mode - (HALF - 1))
    position = position + jnp.where(shifted, shift_y, 0)
    value = wave_sine(wave, mode < HALF, position)
    value = jnp.where(shifted | (mode == 0), value, 2.0 * value)
    high, low = split_bf16(value)
    for part in range(2):
        lanes = slice(part * MODES, (part + 1) * MODES)
        rows_ref[part] = jnp.concatenate([high[:, lanes], high[:, lanes], low[:, lanes]], axis=1)
    mode = lax.broadcasted_iota(jnp.int32, (MODES, COLS), 0)
    wave = jnp.where(mode < HALF, mode, mode - (HALF - 1))
    position = lax.broadcasted_iota(jnp.int32, (MODES, COLS), 1) + first_x
    nest = wave_sine(wave, mode < HALF, position)
    scale = 1.0 / (CELLS * CELLS)
    nest = nest * jnp.where(mode == 0, -scale, -2.0 * scale)
    parent = wave_sine(wave, mode < HALF, position + shift_x)
    nest_high, nest_low = split_bf16(nest)
    parent_high, parent_low = split_bf16(parent)
    even_ref[...] = jnp.concatenate(
        [nest_high, parent_high, nest_high, parent_high, nest_low, parent_low], axis=0
    )
    odd_ref[...] = jnp.concatenate(
        [parent_high, nest_high, parent_high, nest_high, parent_low, nest_low], axis=0
    )


def inverse_tables(place, offset):
    smem = pl.BlockSpec(memory_space=pltpu.SMEM)
    return pl.pallas_call(
        tables_kernel,
        in_specs=[smem, smem],
        out_shape=[
            jax.ShapeDtypeStruct((2, ROWS, 3 * MODES), BF16),
            jax.ShapeDtypeStruct((6 * MODES, COLS), BF16),
            jax.ShapeDtypeStruct((6 * MODES, COLS), BF16),
        ],
        name="inverse_tables",
    )(place, offset)


def inverse_kernel(
    side, steps, place_ref, mask_ref, gain_ref, field_ref, modes_ref, parent_ref, rows_ref, even_ref, odd_ref, *rest
):
    out_ref = rest[-1]
    pairs = field_ref.shape[0]
    core = place_ref[0]
    half = core if side == 0 else 1 - core
    first_pair = half * HALF_PAIRS + pl.program_id(0) * pairs
    lane = lax.broadcasted_iota(jnp.int32, (1, 128), 1)
    is_left = lane < MODES
    left = lax.broadcasted_iota(jnp.int32, (ROWS, 128), 1) < MODES

    def gain(pair, slot):
        slab = 2 * (first_pair + pair) + slot
        field = slab // LEVELS
        level = slab - field * LEVELS
        return gain_ref[field] * mask_ref[level].astype(F32)

    def along_rows(part, first, second):
        high, low = split_bf16(jnp.concatenate([first, second], axis=1))
        stacked = jnp.concatenate([high, low, high], axis=0)
        return jnp.dot(rows_ref[part], stacked, preferred_element_type=F32)

    even, odd = [], []
    for quad in range(pairs // 2):
        nest, parent = [], []
        for pair in (2 * quad, 2 * quad + 1):
            gain_left, gain_right = gain(pair, 0), gain(pair, 1)
            nest.append(modes_ref[pair] * jnp.where(is_left, gain_left, gain_right))
            both = jnp.concatenate([parent_ref[pair, 1], parent_ref[pair, 0]], axis=1)
            parent.append(both * jnp.where(is_left, gain_right, gain_left))
        nest_high, nest_low = split_bf16(along_rows(0, *nest))
        parent_high, parent_low = split_bf16(along_rows(1, *parent))
        for slot in range(2):
            lanes = slice(slot * 128, (slot + 1) * 128)
            nh, nl = nest_high[:, lanes], nest_low[:, lanes]
            ph, pw = parent_high[:, lanes], parent_low[:, lanes]
            high = jnp.where(left, nh, ph)
            even.append(jnp.concatenate([high, jnp.where(left, nl, pw), high], axis=1))
            high = jnp.where(left, ph, nh)
            odd.append(jnp.concatenate([high, jnp.where(left, pw, nl), high], axis=1))
    for slot, (rows, table) in enumerate(((even, even_ref), (odd, odd_ref))):
        correction = jnp.dot(jnp.concatenate(rows, axis=0), table[...], preferred_element_type=F32)
        correction = correction.reshape(pairs, ROWS, COLS)
        out_ref[:, slot] = (field_ref[:, slot].astype(F32) + correction).astype(BF16)


def inverse(side, steps, place, mask, strength, field, modes, parent, tables, previous):
    block = HALF_PAIRS // steps
    smem = pl.BlockSpec(memory_space=pltpu.SMEM)

    def here(i, s):
        half = s[0] if side == 0 else 1 - s[0]
        return (half * steps + i, 0, 0, 0)

    in_specs = [
        smem,
        smem,
        pl.BlockSpec((block, 2, ROWS, COLS), here),
        pl.BlockSpec((block, MODES, 128), lambda i, s: (i, 0, 0)),
        pl.BlockSpec((block, 2, MODES, MODES), here),
        pl.BlockSpec((2, ROWS, 3 * MODES), lambda i, s: (0, 0, 0)),
        pl.BlockSpec((6 * MODES, COLS), lambda i, s: (0, 0)),
        pl.BlockSpec((6 * MODES, COLS), lambda i, s: (0, 0)),
    ]
    operands = [mask, strength, field, modes, parent, *tables]
    aliases = {}
    if previous is not None:
        in_specs.append(pl.BlockSpec(memory_space=pl.ANY))
        operands.append(previous)
        aliases = {len(operands): 0}
    return pl.pallas_call(
        functools.partial(inverse_kernel, side, steps),
        grid_spec=pltpu.PrefetchScalarGridSpec(
            num_scalar_prefetch=1,
            grid=(steps,),
            in_specs=in_specs,
            out_specs=pl.BlockSpec((block, 2, ROWS, COLS), here),
        ),
        out_shape=jax.ShapeDtypeStruct((PAIRS, 2, ROWS, COLS), BF16),
        input_output_aliases=aliases,
        compiler_params=pltpu.CompilerParams(vmem_limit_bytes=VMEM_LIMIT),
        cost_estimate=pl.CostEstimate(
            flops=2 * HALF_PAIRS * 2 * ROWS * COLS * 6 * MODES,
            bytes_accessed=HALF_PAIRS * 2 * ROWS * COLS * 4 + HALF_PAIRS * MODES * 128 * 4,
            transcendentals=0,
        ),
        name="inverse_own" if side == 0 else "inverse_other",
    )(place, *operands)


def device_index(y, core, row):
    return (2 * y + core) * 16 + row


def reduce_groups():
    return [
        [device_index(y, core, row) for y in pair for row in range(16)]
        for core in range(2)
        for pair in ((0, 1), (3, 2))
    ]


CORE_SWAP = [(i, i ^ 1) for i in range(8)]
Y_SWAP = [(2 * y + c, 2 * (3 - y) + c) for y in range(4) for c in range(2)]


def per_device(nest_fields, parent_modes, nest_offset, level_mask, strength):
    index_x = lax.axis_index("gx")
    index_y = lax.axis_index("gy")
    core = index_x & 1
    place = jnp.stack([core, index_x, index_y]).astype(jnp.int32)
    other = jnp.stack([1 - core, index_x, index_y]).astype(jnp.int32)
    field = nest_fields.reshape(PAIRS, 2, ROWS, COLS)
    parent = parent_modes.reshape(PAIRS, 2, MODES, MODES)
    columns, rows = forward_constants()
    columns, rows = jnp.asarray(columns), jnp.asarray(rows)
    groups = reduce_groups()
    members = len(groups[0])

    for_partner = forward(other, field, columns, rows, 2)
    from_partner = lax.ppermute(for_partner, "gx", CORE_SWAP)
    own = forward(place, field, columns, rows, 2)
    own = (own + from_partner).reshape(members, -1, 128)

    def exchange(pieces):
        return lax.all_to_all(pieces, ("gx", "gy"), 0, 0, axis_index_groups=groups, tiled=True)

    piece = exchange(own).sum(0)
    piece = piece + lax.ppermute(piece, "gx", Y_SWAP)
    tables = inverse_tables(place, nest_offset)
    sums = exchange(jnp.broadcast_to(piece[None], (members,) + piece.shape))
    sums = sums.reshape(HALF_PAIRS, MODES, 128)
    other_sums = lax.ppermute(sums, "gx", CORE_SWAP)
    out = inverse(0, 2, place, level_mask, strength, field, sums, parent, tables, None)
    out = inverse(1, 2, place, level_mask, strength, field, other_sums, parent, tables, out)
    return out.reshape(nest_fields.shape)


def solution(mesh):
    in_specs = (P(None, None, "gy", "gx"), P(), P(), P(), P())
    out_specs = P(None, None, "gy", "gx")
    return jax.shard_map(
        per_device, mesh=mesh, in_specs=in_specs, out_specs=out_specs, check_vma=False
    )
```

```python
import functools
import math

import jax
import jax.numpy as jnp
from jax import lax
from jax.experimental import pallas as pl
from jax.experimental.pallas import tpu as pltpu
from jax.sharding import PartitionSpec as P

MODES = 64
HALF = MODES // 2
CELLS = 2048
ROWS = 128
COLS = 256
SLABS = 80
LEVELS = 16
PAIRS = SLABS // 2
HALF_PAIRS = PAIRS // 2
EARLY = HALF_PAIRS // 2
INVERSE_OWN = (10, 10)
INVERSE_OTHER = (8, 8, 4)
HELD = INVERSE_OWN[-1]
TURN = 8
F32 = jnp.float32
BF16 = jnp.bfloat16
VMEM_LIMIT = 16 * 1024 * 1024
VMEM = pl.BlockSpec(memory_space=pltpu.VMEM)
SMEM = pl.BlockSpec(memory_space=pltpu.SMEM)
ANY = pl.BlockSpec(memory_space=pl.ANY)


def split_bf16(value):
    high = value.astype(BF16)
    low = (value - high.astype(F32)).astype(BF16)
    return high, low


def wave_number(mode):
    return jnp.where(mode < HALF, mode, mode - (HALF - 1))


def wave_value(mode, position):
    return wave_sine(wave_number(mode) * position + jnp.where(mode < HALF, CELLS // 4, 0))


def wave_sine(phase):
    phase = ((phase + CELLS // 2) & (CELLS - 1)) - CELLS // 2
    size = jnp.abs(phase)
    size = jnp.minimum(size, CELLS // 2 - size)
    angle = jnp.where(phase < 0, -size, size).astype(F32) * (2.0 * math.pi / CELLS)
    square = angle * angle
    total = jnp.full_like(square, 1.0 / math.factorial(13))
    for degree in (11, 9, 7, 5, 3, 1):
        sign = -1.0 if degree % 4 == 3 else 1.0
        total = total * square + sign / math.factorial(degree)
    return angle * total


def lane_mode(shape):
    return lax.broadcasted_iota(jnp.int32, shape, 1)


def row_index(shape):
    return lax.broadcasted_iota(jnp.int32, shape, 0)


def half_of(side):
    core = lax.axis_index("gx") & 1
    return core if side == 0 else 1 - core


def forward_tables(weight_ref, rows_ref):
    lane = lane_mode((COLS, 128))
    first_x = lax.axis_index("gx") * COLS
    table = wave_value(lane & (MODES - 1), row_index((COLS, 128)) + first_x)
    weight_ref[0:COLS, :] = jnp.where(lane < MODES, table, 0.0).astype(BF16)
    weight_ref[COLS:, :] = jnp.where(lane < MODES, 0.0, table).astype(BF16)
    first_y = lax.axis_index("gy") * ROWS
    shape = (MODES, ROWS)
    high, low = split_bf16(wave_value(row_index(shape), lane_mode(shape) + first_y))
    rows_ref[...] = jnp.concatenate([high, high, low], axis=1)


def forward_columns(tile_ref, source, span, weight_ref, high_ref, low_ref):
    pairs = span.stop - span.start
    left = tile_ref[source, 0].reshape(pairs * ROWS, COLS)
    right = tile_ref[source, 1].reshape(pairs * ROWS, COLS)
    along = jnp.dot(
        jnp.concatenate([left, right], axis=1), weight_ref[...], preferred_element_type=F32
    )
    high, low = split_bf16(along)
    high_ref[span] = high.reshape(pairs, ROWS, 128)
    low_ref[span] = low.reshape(pairs, ROWS, 128)


def forward_rows(span, rows_ref, high_ref, low_ref, out_ref):
    for pair in range(span.start, span.stop, 2):
        high = jnp.concatenate([high_ref[pair], high_ref[pair + 1]], axis=1)
        low = jnp.concatenate([low_ref[pair], low_ref[pair + 1]], axis=1)
        stacked = jnp.concatenate([high, low, high], axis=0)
        sums = jnp.dot(rows_ref[...], stacked, preferred_element_type=F32)
        out_ref[pair] = sums[:, 0:128]
        out_ref[pair + 1] = sums[:, 128:256]


def forward_other_kernel(
    field_ref, out_ref, own_ref, tile_ref, weight_ref, rows_ref, high_ref, low_ref, sems
):
    first_pair = half_of(1) * HALF_PAIRS
    copies = [
        pltpu.make_async_copy(
            field_ref.at[pl.ds(first_pair + index * EARLY, EARLY)],
            tile_ref.at[pl.ds(index * EARLY, EARLY)],
            sems.at[index],
        )
        for index in range(2)
    ]
    copies.append(
        pltpu.make_async_copy(
            field_ref.at[pl.ds(half_of(0) * HALF_PAIRS, EARLY)], own_ref, sems.at[2]
        )
    )
    for copy in copies:
        copy.start()
    forward_tables(weight_ref, rows_ref)
    for index in range(2):
        copies[index].wait()
        span = slice(index * EARLY, (index + 1) * EARLY)
        forward_columns(tile_ref, span, span, weight_ref, high_ref, low_ref)
    forward_rows(slice(0, HALF_PAIRS), rows_ref, high_ref, low_ref, out_ref)
    copies[2].wait()


def forward_own_kernel(
    field_ref, early_ref, out_ref, tile_ref, weight_ref, rows_ref, high_ref, low_ref, sem
):
    late = HALF_PAIRS - EARLY
    first_pair = half_of(0) * HALF_PAIRS + EARLY
    copy = pltpu.make_async_copy(field_ref.at[pl.ds(first_pair, late)], tile_ref, sem)
    copy.start()
    forward_tables(weight_ref, rows_ref)
    early_span, late_span = slice(0, EARLY), slice(EARLY, HALF_PAIRS)
    forward_columns(early_ref, early_span, early_span, weight_ref, high_ref, low_ref)
    forward_rows(early_span, rows_ref, high_ref, low_ref, out_ref)
    copy.wait()
    forward_columns(tile_ref, slice(0, late), late_span, weight_ref, high_ref, low_ref)
    forward_rows(late_span, rows_ref, high_ref, low_ref, out_ref)


def forward(side, field, early=None):
    out_shape = [pltpu.VMEM((HALF_PAIRS, MODES, 128), F32)]
    tile = HALF_PAIRS - EARLY
    if side == 1:
        out_shape.append(pltpu.VMEM((EARLY, 2, ROWS, COLS), BF16))
        tile = HALF_PAIRS
    return pl.pallas_call(
        forward_own_kernel if side == 0 else forward_other_kernel,
        in_specs=[ANY, VMEM] if side == 0 else [ANY],
        out_specs=[VMEM] * len(out_shape),
        out_shape=out_shape,
        scratch_shapes=[
            pltpu.VMEM((tile, 2, ROWS, COLS), BF16),
            pltpu.VMEM((2 * COLS, 128), BF16),
            pltpu.VMEM((MODES, 3 * ROWS), BF16),
            pltpu.VMEM((HALF_PAIRS, ROWS, 128), BF16),
            pltpu.VMEM((HALF_PAIRS, ROWS, 128), BF16),
            pltpu.SemaphoreType.DMA if side == 0 else pltpu.SemaphoreType.DMA((3,)),
        ],
        compiler_params=pltpu.CompilerParams(vmem_limit_bytes=VMEM_LIMIT),
        cost_estimate=pl.CostEstimate(
            flops=2 * HALF_PAIRS * 2 * ROWS * COLS * MODES,
            bytes_accessed=HALF_PAIRS * 2 * ROWS * COLS * 2 + HALF_PAIRS * MODES * 128 * 4,
            transcendentals=0,
        ),
        name="forward_own" if side == 0 else "forward_other",
    )(*([field] if side == 1 else [field, early]))


def turning_table(shift_x):
    shape = (128, 256)
    source, target = row_index(shape), lane_mode(shape)
    source_mode, mode = source & (MODES - 1), target & (MODES - 1)
    same = (source >= MODES) == ((target & 127) >= MODES)
    highest = target >= 128
    wave = jnp.where(highest, HALF, wave_number(mode))
    cosine = wave_sine(wave * shift_x + CELLS // 4)
    sine = wave_sine(wave * shift_x)
    to_cosine = (mode < HALF) & (source_mode == mode + (HALF - 1))
    to_sine = (mode >= HALF) & (source_mode == mode - (HALF - 1)) & (mode != MODES - 1)
    turned = jnp.where(to_cosine, sine, jnp.where(to_sine, -sine, 0.0))
    turned = jnp.where(source_mode == mode, cosine, turned)
    turned = jnp.where(same, turned, 0.0)
    last = jnp.where((source_mode == MODES - 1) & (mode < 3) & jnp.logical_not(same), sine, 0.0)
    return jnp.where(highest, last, turned)


def prepare_kernel(
    scalar_ref,
    parent_ref,
    after_ref,
    rows_ref,
    even_ref,
    odd_ref,
    gain_ref,
    along_ref,
    last_ref,
):
    del after_ref
    first_x = lax.axis_index("gx") * COLS
    first_y = lax.axis_index("gy") * ROWS
    shift_x = scalar_ref[0].astype(jnp.int32)
    shift_y = scalar_ref[1].astype(jnp.int32)
    shape = (ROWS, 128)
    lane = lane_mode(shape)
    mode = lane & (MODES - 1)
    position = row_index(shape) + first_y + jnp.where(lane < MODES, 0, shift_y)
    value = wave_value(mode, position)
    value = jnp.where((lane >= MODES) | (mode == 0), value, 2.0 * value)
    high, low = split_bf16(value)
    nest, parent = slice(0, MODES), slice(MODES, 128)
    rows_ref[...] = jnp.concatenate([high[:, nest], high[:, nest], low[:, nest]], axis=1)
    parent_rows = jnp.concatenate([high[:, parent], high[:, parent], low[:, parent]], axis=1)
    shape = (MODES, COLS)
    position = lane_mode(shape) + first_x
    high, low = split_bf16(wave_value(row_index(shape), position))
    highest = wave_sine(HALF * position + CELLS // 4)
    highest_high, highest_low = split_bf16(highest)
    row = row_index(shape)
    zero = jnp.zeros(shape, BF16)
    extra = jnp.where(row < 2, highest_high, jnp.where(row == 2, highest_low, zero))
    even_ref[...] = jnp.concatenate([high, high, low, extra], axis=0)
    odd_ref[...] = jnp.concatenate([high, high, extra, low], axis=0)
    high, low = split_bf16(turning_table(shift_x))
    turning = jnp.concatenate([high, high, low], axis=0)

    left = lane_mode((1, 128)) < MODES
    scale = jnp.where(lane_mode((1, 128)) & (MODES - 1) == 0, -1.0, -2.0) / (CELLS * CELLS)
    is_low = lane_mode((ROWS, 256)) & (MODES - 1) == 1
    for start in range(0, PAIRS, TURN):
        rows = []
        for pair in range(start, start + TURN):
            field, level = divmod(2 * pair, LEVELS)
            strength = scalar_ref[18 + field]
            gain = jnp.where(
                left, strength * scalar_ref[2 + level], strength * scalar_ref[3 + level]
            )
            gain_ref[pair : pair + 1, :] = gain * scale
            both = jnp.concatenate([parent_ref[pair, 0], parent_ref[pair, 1]], axis=1) * gain
            high, low = split_bf16(both)
            rows.append(jnp.concatenate([high, low, high], axis=1))
        turned = jnp.dot(jnp.concatenate(rows, axis=0), turning, preferred_element_type=F32)
        for pair in range(0, TURN, 2):
            first = turned[pair * MODES : (pair + 1) * MODES]
            second = turned[(pair + 1) * MODES : (pair + 2) * MODES]
            high, low = split_bf16(jnp.concatenate([first[:, 0:128], second[:, 0:128]], axis=1))
            stacked = jnp.concatenate([high, low, high], axis=0)
            along = jnp.dot(parent_rows, stacked, preferred_element_type=F32)
            high, low = split_bf16(jnp.concatenate([first[:, 128:], second[:, 128:]], axis=1))
            stacked = jnp.concatenate([high, low, high], axis=0)
            high, low = split_bf16(jnp.dot(parent_rows, stacked, preferred_element_type=F32))
            last = jnp.where(is_low, low, high)
            for slot in range(2):
                lanes = slice(slot * 128, (slot + 1) * 128)
                along_ref[start + pair + slot] = along[:, lanes]
                last_ref[start + pair + slot] = last[:, lanes]


def prepare(scalars, parent, after):
    return pl.pallas_call(
        prepare_kernel,
        in_specs=[SMEM, VMEM, ANY],
        out_specs=[VMEM] * 6,
        out_shape=[
            jax.ShapeDtypeStruct((ROWS, 3 * MODES), BF16),
            jax.ShapeDtypeStruct((4 * MODES, COLS), BF16),
            jax.ShapeDtypeStruct((4 * MODES, COLS), BF16),
            jax.ShapeDtypeStruct((PAIRS, 128), F32),
            jax.ShapeDtypeStruct((PAIRS, ROWS, 128), F32),
            jax.ShapeDtypeStruct((PAIRS, ROWS, 128), BF16),
        ],
        compiler_params=pltpu.CompilerParams(vmem_limit_bytes=VMEM_LIMIT),
        cost_estimate=pl.CostEstimate(
            flops=20 * PAIRS * ROWS * 128 * 3 * MODES,
            bytes_accessed=PAIRS * MODES * 128 * 8,
            transcendentals=0,
        ),
        name="parent_along_rows",
    )(scalars, parent, after)


def inverse_kernel(
    side, modes_ref, field_ref, rows_ref, even_ref, odd_ref, gain_ref, along_ref, last_ref, *rest
):
    first_pair = half_of(side) * HALF_PAIRS
    copies = []
    if side == 0:
        out_ref, held_ref, result_ref, left_ref, sems = rest
        chunks = INVERSE_OWN
    else:
        held_ref, _, out_ref, result_ref, left_ref, sems = rest
        chunks = INVERSE_OTHER
        first_held = half_of(0) * HALF_PAIRS + HALF_PAIRS - HELD
        copies.append(
            pltpu.make_async_copy(
                held_ref, out_ref.at[pl.ds(first_held, HELD)], sems.at[len(chunks)]
            )
        )
        copies[0].start()
    left = lane_mode((ROWS, 128)) < MODES
    for here in range(0, HALF_PAIRS, 2):
        nest = []
        for pair in (here, here + 1):
            nest.append(modes_ref[pair] * gain_ref[pl.ds(first_pair + pair, 1), :])
        high, low = split_bf16(jnp.concatenate(nest, axis=1))
        stacked = jnp.concatenate([high, low, high], axis=0)
        nest = jnp.dot(rows_ref[...], stacked, preferred_element_type=F32)
        for slot in range(2):
            pair = here + slot
            both = nest[:, slot * 128 : (slot + 1) * 128] + along_ref[first_pair + pair]
            high = both.astype(BF16)
            low = pltpu.roll(both - high.astype(F32), MODES, 1).astype(BF16)
            last = last_ref[first_pair + pair]
            left_ref[0, pair, :, 0:128] = jnp.where(left, high, low)
            left_ref[0, pair, :, 128:256] = jnp.where(left, high, last)
            left_ref[1, pair, :, 0:128] = jnp.where(left, low, high)
            left_ref[1, pair, :, 128:256] = jnp.where(left, last, high)
    start = 0
    for index, chunk in enumerate(chunks):
        span = slice(start, start + chunk)
        held = side == 0 and index == len(chunks) - 1
        for slot, table in enumerate((even_ref, odd_ref)):
            rows = left_ref[slot, span].reshape(chunk * ROWS, 256)
            correction = jnp.dot(rows, table[...], preferred_element_type=F32)
            correction = correction.reshape(chunk, ROWS, COLS)
            nudged = field_ref[pl.ds(first_pair + start, chunk), slot].astype(F32) + correction
            if held:
                held_ref[:, slot] = nudged.astype(BF16)
            else:
                result_ref[span, slot] = nudged.astype(BF16)
        if not held:
            copies.append(
                pltpu.make_async_copy(
                    result_ref.at[pl.ds(start, chunk)],
                    out_ref.at[pl.ds(first_pair + start, chunk)],
                    sems.at[index],
                )
            )
            copies[-1].start()
        start += chunk
    for copy in copies:
        copy.wait()


def inverse(side, modes, field, prepared, previous):
    operands = [modes, field, *prepared]
    in_specs = [VMEM] * len(operands)
    out_specs = [ANY]
    out_shape = [jax.ShapeDtypeStruct((PAIRS, 2, ROWS, COLS), BF16)]
    aliases = {}
    if side == 0:
        out_specs.append(VMEM)
        out_shape.append(pltpu.VMEM((HELD, 2, ROWS, COLS), BF16))
    else:
        out, held = previous
        operands += [held, out]
        in_specs += [VMEM, ANY]
        aliases = {len(operands) - 1: 0}
    return pl.pallas_call(
        functools.partial(inverse_kernel, side),
        in_specs=in_specs,
        out_specs=out_specs,
        out_shape=out_shape,
        scratch_shapes=[
            pltpu.VMEM((HALF_PAIRS, 2, ROWS, COLS), BF16),
            pltpu.VMEM((2, HALF_PAIRS, ROWS, 256), BF16),
            pltpu.SemaphoreType.DMA((4,)),
        ],
        input_output_aliases=aliases,
        compiler_params=pltpu.CompilerParams(vmem_limit_bytes=VMEM_LIMIT),
        cost_estimate=pl.CostEstimate(
            flops=2 * HALF_PAIRS * 2 * ROWS * COLS * 4 * MODES,
            bytes_accessed=HALF_PAIRS * 2 * ROWS * COLS * 4 + HALF_PAIRS * MODES * 128 * 4,
            transcendentals=0,
        ),
        name="inverse_own" if side == 0 else "inverse_other",
    )(*operands)


def device_index(y, core, row):
    return (2 * y + core) * 16 + row


def reduce_groups():
    return [
        [device_index(y, core, row) for y in pair for row in range(16)]
        for core in range(2)
        for pair in ((0, 1), (3, 2))
    ]


CORE_SWAP = [(i, i ^ 1) for i in range(8)]
Y_SWAP = [(2 * y + c, 2 * (3 - y) + c) for y in range(4) for c in range(2)]


def per_device(nest_fields, parent_modes, nest_offset, level_mask, strength):
    field = nest_fields.reshape(PAIRS, 2, ROWS, COLS)
    field = pltpu.with_memory_space_constraint(field, pltpu.HBM)
    parent = parent_modes.reshape(PAIRS, 2, MODES, MODES)
    scalars = jnp.concatenate([nest_offset.astype(F32), level_mask.astype(F32), strength])
    groups = reduce_groups()
    members = len(groups[0])

    for_partner, early = forward(1, field)
    from_partner = lax.ppermute(for_partner, "gx", CORE_SWAP)
    (own,) = forward(0, field, early)
    own = (own + from_partner).reshape(members, -1, 128)
    own, scalars = lax.optimization_barrier((own, scalars))

    def exchange(pieces):
        return lax.all_to_all(pieces, ("gx", "gy"), 0, 0, axis_index_groups=groups, tiled=True)

    piece = exchange(own).sum(0)
    from_pair = lax.ppermute(piece, "gx", Y_SWAP)
    prepared = prepare(scalars, parent, piece)
    from_pair, *prepared = lax.optimization_barrier((from_pair, *prepared))
    piece = piece + from_pair
    sums = exchange(jnp.broadcast_to(piece[None], (members,) + piece.shape))
    sums = sums.reshape(HALF_PAIRS, MODES, 128)
    other_sums = lax.ppermute(sums, "gx", CORE_SWAP)
    whole = nest_fields.reshape(PAIRS, 2, ROWS, COLS)
    previous = inverse(0, sums, whole, prepared, None)
    (out,) = inverse(1, other_sums, whole, prepared, previous)
    return out.reshape(nest_fields.shape)


def solution(mesh):
    in_specs = (P(None, None, "gy", "gx"), P(), P(), P(), P())
    out_specs = P(None, None, "gy", "gx")
    return jax.shard_map(
        per_device, mesh=mesh, in_specs=in_specs, out_specs=out_specs, check_vma=False
    )
```

```python
import functools
import math

import jax
import jax.numpy as jnp
from jax import lax
from jax.experimental import pallas as pl
from jax.experimental.pallas import tpu as pltpu
from jax.sharding import PartitionSpec as P

MODES = 64
HALF = MODES // 2
CELLS = 2048
ROWS = 128
COLS = 256
SLABS = 80
LEVELS = 16
PAIRS = SLABS // 2
HALF_PAIRS = PAIRS // 2
INVERSE_OWN = (6, 8, 6)
INVERSE_OTHER = (10, 6, 4)
HELD = INVERSE_OWN[-1]
TURN = 8
F32 = jnp.float32
BF16 = jnp.bfloat16
VMEM_LIMIT = 16 * 1024 * 1024
VMEM = pl.BlockSpec(memory_space=pltpu.VMEM)
SMEM = pl.BlockSpec(memory_space=pltpu.SMEM)
ANY = pl.BlockSpec(memory_space=pl.ANY)


def split_bf16(value):
    high = value.astype(BF16)
    low = (value - high.astype(F32)).astype(BF16)
    return high, low


def wave_number(mode):
    return jnp.where(mode < HALF, mode, mode - (HALF - 1))


def wave_value(mode, position):
    return wave_sine(wave_number(mode) * position + jnp.where(mode < HALF, CELLS // 4, 0))


def wave_sine(phase):
    phase = ((phase + CELLS // 2) & (CELLS - 1)) - CELLS // 2
    size = jnp.abs(phase)
    size = jnp.minimum(size, CELLS // 2 - size)
    angle = jnp.where(phase < 0, -size, size).astype(F32) * (2.0 * math.pi / CELLS)
    square = angle * angle
    total = jnp.full_like(square, 1.0 / math.factorial(13))
    for degree in (11, 9, 7, 5, 3, 1):
        sign = -1.0 if degree % 4 == 3 else 1.0
        total = total * square + sign / math.factorial(degree)
    return angle * total


def lane_mode(shape):
    return lax.broadcasted_iota(jnp.int32, shape, 1)


def row_index(shape):
    return lax.broadcasted_iota(jnp.int32, shape, 0)


def half_of(side):
    core = lax.axis_index("gx") & 1
    return core if side == 0 else 1 - core


def forward_tables(weight_ref, rows_ref):
    lane = lane_mode((COLS, 128))
    first_x = lax.axis_index("gx") * COLS
    table = wave_value(lane & (MODES - 1), row_index((COLS, 128)) + first_x)
    weight_ref[0:COLS, :] = jnp.where(lane < MODES, table, 0.0).astype(BF16)
    weight_ref[COLS:, :] = jnp.where(lane < MODES, 0.0, table).astype(BF16)
    first_y = lax.axis_index("gy") * ROWS
    shape = (MODES, ROWS)
    high, low = split_bf16(wave_value(row_index(shape), lane_mode(shape) + first_y))
    rows_ref[...] = jnp.concatenate([high, high, low], axis=1)


def forward_columns(tile_ref, span, weight_ref, high_ref, low_ref):
    pairs = span.stop - span.start
    left = tile_ref[span, 0].reshape(pairs * ROWS, COLS)
    right = tile_ref[span, 1].reshape(pairs * ROWS, COLS)
    along = jnp.dot(
        jnp.concatenate([left, right], axis=1), weight_ref[...], preferred_element_type=F32
    )
    high, low = split_bf16(along)
    high_ref[span] = high.reshape(pairs, ROWS, 128)
    low_ref[span] = low.reshape(pairs, ROWS, 128)


def forward_rows(rows_ref, high_ref, low_ref, out_ref):
    for pair in range(0, HALF_PAIRS, 2):
        high = jnp.concatenate([high_ref[pair], high_ref[pair + 1]], axis=1)
        low = jnp.concatenate([low_ref[pair], low_ref[pair + 1]], axis=1)
        stacked = jnp.concatenate([high, low, high], axis=0)
        sums = jnp.dot(rows_ref[...], stacked, preferred_element_type=F32)
        out_ref[pair] = sums[:, 0:128]
        out_ref[pair + 1] = sums[:, 128:256]


def forward_other_kernel(
    field_ref, out_ref, own_ref, tile_ref, weight_ref, rows_ref, high_ref, low_ref, sems
):
    first_pair = half_of(1) * HALF_PAIRS
    chunk = HALF_PAIRS // 2
    copies = [
        pltpu.make_async_copy(
            field_ref.at[pl.ds(first_pair + index * chunk, chunk)],
            tile_ref.at[pl.ds(index * chunk, chunk)],
            sems.at[index],
        )
        for index in range(2)
    ]
    copies.append(
        pltpu.make_async_copy(
            field_ref.at[pl.ds(half_of(0) * HALF_PAIRS, HALF_PAIRS)], own_ref, sems.at[2]
        )
    )
    for copy in copies:
        copy.start()
    forward_tables(weight_ref, rows_ref)
    for index in range(2):
        copies[index].wait()
        span = slice(index * chunk, (index + 1) * chunk)
        forward_columns(tile_ref, span, weight_ref, high_ref, low_ref)
    forward_rows(rows_ref, high_ref, low_ref, out_ref)
    copies[2].wait()


def forward_own_kernel(tile_ref, out_ref, weight_ref, rows_ref, high_ref, low_ref):
    forward_tables(weight_ref, rows_ref)
    forward_columns(tile_ref, slice(0, HALF_PAIRS), weight_ref, high_ref, low_ref)
    forward_rows(rows_ref, high_ref, low_ref, out_ref)


def forward(side, field):
    tile = (HALF_PAIRS, 2, ROWS, COLS)
    out_shape = [pltpu.VMEM((HALF_PAIRS, MODES, 128), F32)]
    scratch = [
        pltpu.VMEM((2 * COLS, 128), BF16),
        pltpu.VMEM((MODES, 3 * ROWS), BF16),
        pltpu.VMEM((HALF_PAIRS, ROWS, 128), BF16),
        pltpu.VMEM((HALF_PAIRS, ROWS, 128), BF16),
    ]
    if side == 1:
        out_shape.append(pltpu.VMEM(tile, BF16))
        scratch = [pltpu.VMEM(tile, BF16), *scratch, pltpu.SemaphoreType.DMA((3,))]
    return pl.pallas_call(
        forward_own_kernel if side == 0 else forward_other_kernel,
        in_specs=[VMEM if side == 0 else ANY],
        out_specs=[VMEM] * len(out_shape),
        out_shape=out_shape,
        scratch_shapes=scratch,
        compiler_params=pltpu.CompilerParams(vmem_limit_bytes=VMEM_LIMIT),
        cost_estimate=pl.CostEstimate(
            flops=2 * HALF_PAIRS * 2 * ROWS * COLS * MODES,
            bytes_accessed=HALF_PAIRS * 2 * ROWS * COLS * 2 + HALF_PAIRS * MODES * 128 * 4,
            transcendentals=0,
        ),
        name="forward_own" if side == 0 else "forward_other",
    )(field)


def turning_table(shift_x):
    shape = (128, 256)
    source, target = row_index(shape), lane_mode(shape)
    source_mode, mode = source & (MODES - 1), target & (MODES - 1)
    same = (source >= MODES) == ((target & 127) >= MODES)
    highest = target >= 128
    wave = jnp.where(highest, HALF, wave_number(mode))
    cosine = wave_sine(wave * shift_x + CELLS // 4)
    sine = wave_sine(wave * shift_x)
    to_cosine = (mode < HALF) & (source_mode == mode + (HALF - 1))
    to_sine = (mode >= HALF) & (source_mode == mode - (HALF - 1)) & (mode != MODES - 1)
    turned = jnp.where(to_cosine, sine, jnp.where(to_sine, -sine, 0.0))
    turned = jnp.where(source_mode == mode, cosine, turned)
    turned = jnp.where(same, turned, 0.0)
    last = jnp.where((source_mode == MODES - 1) & (mode < 3) & jnp.logical_not(same), sine, 0.0)
    return jnp.where(highest, last, turned)


def tables_kernel(
    scalar_ref, after_ref, rows_ref, parent_rows_ref, even_ref, odd_ref, turning_ref, gain_ref
):
    del after_ref
    first_x = lax.axis_index("gx") * COLS
    first_y = lax.axis_index("gy") * ROWS
    shift_x = scalar_ref[0].astype(jnp.int32)
    shift_y = scalar_ref[1].astype(jnp.int32)
    shape = (ROWS, 128)
    lane = lane_mode(shape)
    mode = lane & (MODES - 1)
    position = row_index(shape) + first_y + jnp.where(lane < MODES, 0, shift_y)
    value = wave_value(mode, position)
    value = jnp.where((lane >= MODES) | (mode == 0), value, 2.0 * value)
    high, low = split_bf16(value)
    nest, parent = slice(0, MODES), slice(MODES, 128)
    rows_ref[...] = jnp.concatenate([high[:, nest], high[:, nest], low[:, nest]], axis=1)
    parent_rows_ref[...] = jnp.concatenate(
        [high[:, parent], high[:, parent], low[:, parent]], axis=1
    )
    shape = (MODES, COLS)
    position = lane_mode(shape) + first_x
    high, low = split_bf16(wave_value(row_index(shape), position))
    highest = wave_sine(HALF * position + CELLS // 4)
    highest_high, highest_low = split_bf16(highest)
    row = row_index(shape)
    zero = jnp.zeros(shape, BF16)
    extra = jnp.where(row < 2, highest_high, jnp.where(row == 2, highest_low, zero))
    even_ref[...] = jnp.concatenate([high, high, low, extra], axis=0)
    odd_ref[...] = jnp.concatenate([high, high, extra, low], axis=0)
    high, low = split_bf16(turning_table(shift_x))
    turning_ref[...] = jnp.concatenate([high, high, low], axis=0)
    left = lane_mode((1, 128)) < MODES
    for pair in range(PAIRS):
        field, level = divmod(2 * pair, LEVELS)
        strength = scalar_ref[18 + field]
        gain_ref[pair : pair + 1, :] = jnp.where(
            left, strength * scalar_ref[2 + level], strength * scalar_ref[3 + level]
        )


def parent_kernel(
    parent_ref, after_ref, parent_rows_ref, turning_ref, gain_ref, scaled_ref, along_ref, last_ref
):
    del after_ref
    mode = lane_mode((PAIRS, 128)) & (MODES - 1)
    scaled_ref[...] = gain_ref[...] * (jnp.where(mode == 0, -1.0, -2.0) / (CELLS * CELLS))
    is_low = lane_mode((ROWS, 256)) & (MODES - 1) == 1
    for start in range(0, PAIRS, TURN):
        rows = []
        for pair in range(start, start + TURN):
            both = jnp.concatenate([parent_ref[pair, 0], parent_ref[pair, 1]], axis=1)
            high, low = split_bf16(both * gain_ref[pair : pair + 1, :])
            rows.append(jnp.concatenate([high, low, high], axis=1))
        turned = jnp.dot(
            jnp.concatenate(rows, axis=0), turning_ref[...], preferred_element_type=F32
        )
        for pair in range(0, TURN, 2):
            first = turned[pair * MODES : (pair + 1) * MODES]
            second = turned[(pair + 1) * MODES : (pair + 2) * MODES]
            high, low = split_bf16(jnp.concatenate([first[:, 0:128], second[:, 0:128]], axis=1))
            stacked = jnp.concatenate([high, low, high], axis=0)
            along = jnp.dot(parent_rows_ref[...], stacked, preferred_element_type=F32)
            high, low = split_bf16(jnp.concatenate([first[:, 128:], second[:, 128:]], axis=1))
            stacked = jnp.concatenate([high, low, high], axis=0)
            last = jnp.dot(parent_rows_ref[...], stacked, preferred_element_type=F32)
            high, low = split_bf16(last)
            last = jnp.where(is_low, low, high)
            for slot in range(2):
                lanes = slice(slot * 128, (slot + 1) * 128)
                along_ref[start + pair + slot] = along[:, lanes]
                last_ref[start + pair + slot] = last[:, lanes]


def make_tables(scalars, after):
    return pl.pallas_call(
        tables_kernel,
        in_specs=[SMEM, ANY],
        out_specs=[VMEM] * 6,
        out_shape=[
            jax.ShapeDtypeStruct((ROWS, 3 * MODES), BF16),
            jax.ShapeDtypeStruct((ROWS, 3 * MODES), BF16),
            jax.ShapeDtypeStruct((4 * MODES, COLS), BF16),
            jax.ShapeDtypeStruct((4 * MODES, COLS), BF16),
            jax.ShapeDtypeStruct((6 * MODES, 256), BF16),
            jax.ShapeDtypeStruct((PAIRS, 128), F32),
        ],
        compiler_params=pltpu.CompilerParams(vmem_limit_bytes=VMEM_LIMIT),
        name="tables",
    )(scalars, after)


def parent_along_rows(parent, after, parent_rows, turning, gain):
    return pl.pallas_call(
        parent_kernel,
        in_specs=[VMEM, ANY, VMEM, VMEM, VMEM],
        out_specs=[VMEM] * 3,
        out_shape=[
            jax.ShapeDtypeStruct((PAIRS, 128), F32),
            jax.ShapeDtypeStruct((PAIRS, ROWS, 128), F32),
            jax.ShapeDtypeStruct((PAIRS, ROWS, 128), BF16),
        ],
        compiler_params=pltpu.CompilerParams(vmem_limit_bytes=VMEM_LIMIT),
        cost_estimate=pl.CostEstimate(
            flops=20 * PAIRS * ROWS * 128 * 3 * MODES,
            bytes_accessed=PAIRS * MODES * 128 * 8,
            transcendentals=0,
        ),
        name="parent_along_rows",
    )(parent, after, parent_rows, turning, gain)


def inverse_kernel(
    side, modes_ref, field_ref, rows_ref, even_ref, odd_ref, gain_ref, along_ref, last_ref, *rest
):
    first_pair = half_of(side) * HALF_PAIRS
    copies = []
    if side == 0:
        out_ref, held_ref, result_ref, left_ref, sems = rest
        chunks = INVERSE_OWN
    else:
        held_ref, _, out_ref, result_ref, left_ref, sems = rest
        chunks = INVERSE_OTHER
        first_held = half_of(0) * HALF_PAIRS + HALF_PAIRS - HELD
        copies.append(
            pltpu.make_async_copy(
                held_ref, out_ref.at[pl.ds(first_held, HELD)], sems.at[len(chunks)]
            )
        )
        copies[0].start()
    left = lane_mode((ROWS, 128)) < MODES
    start = 0
    for index, chunk in enumerate(chunks):
        span = slice(start, start + chunk)
        for here in range(start, start + chunk, 2):
            nest = []
            for pair in (here, here + 1):
                nest.append(modes_ref[pair] * gain_ref[pl.ds(first_pair + pair, 1), :])
            high, low = split_bf16(jnp.concatenate(nest, axis=1))
            stacked = jnp.concatenate([high, low, high], axis=0)
            nest = jnp.dot(rows_ref[...], stacked, preferred_element_type=F32)
            for slot in range(2):
                pair = here + slot
                both = nest[:, slot * 128 : (slot + 1) * 128] + along_ref[first_pair + pair]
                high = both.astype(BF16)
                low = pltpu.roll(both - high.astype(F32), MODES, 1).astype(BF16)
                last = last_ref[first_pair + pair]
                left_ref[0, pair, :, 0:128] = jnp.where(left, high, low)
                left_ref[0, pair, :, 128:256] = jnp.where(left, high, last)
                left_ref[1, pair, :, 0:128] = jnp.where(left, low, high)
                left_ref[1, pair, :, 128:256] = jnp.where(left, last, high)
        held = side == 0 and index == len(chunks) - 1
        for slot, table in enumerate((even_ref, odd_ref)):
            rows = left_ref[slot, span].reshape(chunk * ROWS, 256)
            correction = jnp.dot(rows, table[...], preferred_element_type=F32)
            correction = correction.reshape(chunk, ROWS, COLS)
            nudged = field_ref[pl.ds(first_pair + start, chunk), slot].astype(F32) + correction
            if held:
                held_ref[:, slot] = nudged.astype(BF16)
            else:
                result_ref[span, slot] = nudged.astype(BF16)
        if not held:
            copies.append(
                pltpu.make_async_copy(
                    result_ref.at[pl.ds(start, chunk)],
                    out_ref.at[pl.ds(first_pair + start, chunk)],
                    sems.at[index],
                )
            )
            copies[-1].start()
        start += chunk
    for copy in copies:
        copy.wait()


def inverse(side, modes, field, prepared, previous):
    operands = [modes, field, *prepared]
    in_specs = [VMEM] * len(operands)
    out_specs = [ANY]
    out_shape = [jax.ShapeDtypeStruct((PAIRS, 2, ROWS, COLS), BF16)]
    aliases = {}
    if side == 0:
        out_specs.append(VMEM)
        out_shape.append(pltpu.VMEM((HELD, 2, ROWS, COLS), BF16))
    else:
        out, held = previous
        operands += [held, out]
        in_specs += [VMEM, ANY]
        aliases = {len(operands) - 1: 0}
    return pl.pallas_call(
        functools.partial(inverse_kernel, side),
        in_specs=in_specs,
        out_specs=out_specs,
        out_shape=out_shape,
        scratch_shapes=[
            pltpu.VMEM((HALF_PAIRS, 2, ROWS, COLS), BF16),
            pltpu.VMEM((2, HALF_PAIRS, ROWS, 256), BF16),
            pltpu.SemaphoreType.DMA((4,)),
        ],
        input_output_aliases=aliases,
        compiler_params=pltpu.CompilerParams(vmem_limit_bytes=VMEM_LIMIT),
        cost_estimate=pl.CostEstimate(
            flops=2 * HALF_PAIRS * 2 * ROWS * COLS * 4 * MODES,
            bytes_accessed=HALF_PAIRS * 2 * ROWS * COLS * 4 + HALF_PAIRS * MODES * 128 * 4,
            transcendentals=0,
        ),
        name="inverse_own" if side == 0 else "inverse_other",
    )(*operands)


def reduce_groups():
    return [
        [(2 * y + core) * 16 + 4 * z + x for z in pair for y in range(4) for x in range(4)]
        for core in range(2)
        for pair in ((0, 1), (3, 2))
    ]


CORE_SWAP = [(i, i ^ 1) for i in range(8)]
Z_SWAP = [(4 * z + x, 4 * (3 - z) + x) for z in range(4) for x in range(4)]


def sum_kernel(pieces_ref, out_ref):
    out_ref[...] = jnp.sum(pieces_ref[...], axis=0)


def sum_pieces(pieces):
    return pl.pallas_call(
        sum_kernel,
        in_specs=[VMEM],
        out_specs=VMEM,
        out_shape=pltpu.VMEM(pieces.shape[1:], F32),
        compiler_params=pltpu.CompilerParams(vmem_limit_bytes=VMEM_LIMIT),
        name="sum_pieces",
    )(pltpu.with_memory_space_constraint(pieces, pltpu.VMEM))


def per_device(nest_fields, parent_modes, nest_offset, level_mask, strength):
    field = nest_fields.reshape(PAIRS, 2, ROWS, COLS)
    field = pltpu.with_memory_space_constraint(field, pltpu.HBM)
    parent = parent_modes.reshape(PAIRS, 2, MODES, MODES)
    scalars = jnp.concatenate([nest_offset.astype(F32), level_mask.astype(F32), strength])
    groups = reduce_groups()
    members = len(groups[0])

    for_partner, own_tile = forward(1, field)
    from_partner = lax.ppermute(for_partner, "gx", CORE_SWAP)
    (own,) = forward(0, own_tile)
    tables = make_tables(scalars, own)
    from_partner, tables = lax.optimization_barrier((from_partner, tables))
    rows, parent_rows, even, odd, turning, gain = tables
    own = (own + from_partner).reshape(members, -1, 128)

    def exchange(pieces):
        return lax.all_to_all(pieces, ("gx", "gy"), 0, 0, axis_index_groups=groups, tiled=True)

    piece = sum_pieces(exchange(own))
    from_pair = lax.ppermute(piece, "gy", Z_SWAP)
    parents = parent_along_rows(parent, piece, parent_rows, turning, gain)
    from_pair, parents = lax.optimization_barrier((from_pair, parents))
    prepared = [rows, even, odd, *parents]
    piece = piece + from_pair
    sums = exchange(jnp.broadcast_to(piece[None], (members,) + piece.shape))
    sums = sums.reshape(HALF_PAIRS, MODES, 128)
    other_sums = lax.ppermute(sums, "gx", CORE_SWAP)
    whole = nest_fields.reshape(PAIRS, 2, ROWS, COLS)
    previous = inverse(0, sums, whole, prepared, None)
    (out,) = inverse(1, other_sums, whole, prepared, previous)
    return out.reshape(nest_fields.shape)


def solution(mesh):
    in_specs = (P(None, None, "gy", "gx"), P(), P(), P(), P())
    out_specs = P(None, None, "gy", "gx")
    return jax.shard_map(
        per_device, mesh=mesh, in_specs=in_specs, out_specs=out_specs, check_vma=False
    )
```

```python
import functools
import math

import jax
import jax.numpy as jnp
from jax import lax
from jax.experimental import pallas as pl
from jax.experimental.pallas import tpu as pltpu
from jax.sharding import PartitionSpec as P

MODES = 64
HALF = MODES // 2
CELLS = 2048
ROWS = 128
COLS = 256
SLABS = 80
LEVELS = 16
PAIRS = SLABS // 2
HALF_PAIRS = PAIRS // 2
INVERSE_OWN = (6, 8, 6)
INVERSE_OTHER = (10, 6, 4)
HELD = INVERSE_OWN[-1]
TURN = 8
F32 = jnp.float32
BF16 = jnp.bfloat16
VMEM_LIMIT = 16 * 1024 * 1024
VMEM = pl.BlockSpec(memory_space=pltpu.VMEM)
SMEM = pl.BlockSpec(memory_space=pltpu.SMEM)
ANY = pl.BlockSpec(memory_space=pl.ANY)


def split_bf16(value):
    high = value.astype(BF16)
    low = (value - high.astype(F32)).astype(BF16)
    return high, low


def wave_number(mode):
    return jnp.where(mode < HALF, mode, mode - (HALF - 1))


def wave_value(mode, position):
    return wave_sine(wave_number(mode) * position + jnp.where(mode < HALF, CELLS // 4, 0))


def wave_sine(phase):
    phase = ((phase + CELLS // 2) & (CELLS - 1)) - CELLS // 2
    size = jnp.abs(phase)
    size = jnp.minimum(size, CELLS // 2 - size)
    angle = jnp.where(phase < 0, -size, size).astype(F32) * (2.0 * math.pi / CELLS)
    square = angle * angle
    total = jnp.full_like(square, 1.0 / math.factorial(13))
    for degree in (11, 9, 7, 5, 3, 1):
        sign = -1.0 if degree % 4 == 3 else 1.0
        total = total * square + sign / math.factorial(degree)
    return angle * total


def lane_mode(shape):
    return lax.broadcasted_iota(jnp.int32, shape, 1)


def row_index(shape):
    return lax.broadcasted_iota(jnp.int32, shape, 0)


def half_of(side):
    core = lax.axis_index("gx") & 1
    return core if side == 0 else 1 - core


def forward_tables(weight_ref, rows_ref):
    lane = lane_mode((COLS, 128))
    first_x = lax.axis_index("gx") * COLS
    table = wave_value(lane & (MODES - 1), row_index((COLS, 128)) + first_x)
    weight_ref[0:COLS, :] = jnp.where(lane < MODES, table, 0.0).astype(BF16)
    weight_ref[COLS:, :] = jnp.where(lane < MODES, 0.0, table).astype(BF16)
    first_y = lax.axis_index("gy") * ROWS
    shape = (MODES, ROWS)
    high, low = split_bf16(wave_value(row_index(shape), lane_mode(shape) + first_y))
    rows_ref[...] = jnp.concatenate([high, high, low], axis=1)


def forward_columns(tile_ref, span, weight_ref, high_ref, low_ref):
    pairs = span.stop - span.start
    left = tile_ref[span, 0].reshape(pairs * ROWS, COLS)
    right = tile_ref[span, 1].reshape(pairs * ROWS, COLS)
    along = jnp.dot(
        jnp.concatenate([left, right], axis=1), weight_ref[...], preferred_element_type=F32
    )
    high, low = split_bf16(along)
    high_ref[span] = high.reshape(pairs, ROWS, 128)
    low_ref[span] = low.reshape(pairs, ROWS, 128)


def forward_rows(rows_ref, high_ref, low_ref, out_ref):
    for pair in range(0, HALF_PAIRS, 2):
        high = jnp.concatenate([high_ref[pair], high_ref[pair + 1]], axis=1)
        low = jnp.concatenate([low_ref[pair], low_ref[pair + 1]], axis=1)
        stacked = jnp.concatenate([high, low, high], axis=0)
        sums = jnp.dot(rows_ref[...], stacked, preferred_element_type=F32)
        out_ref[pair] = sums[:, 0:128]
        out_ref[pair + 1] = sums[:, 128:256]


def forward_other_kernel(
    field_ref, out_ref, own_ref, tile_ref, weight_ref, rows_ref, high_ref, low_ref, sems
):
    first_pair = half_of(1) * HALF_PAIRS
    chunk = HALF_PAIRS // 2
    copies = [
        pltpu.make_async_copy(
            field_ref.at[pl.ds(first_pair + index * chunk, chunk)],
            tile_ref.at[pl.ds(index * chunk, chunk)],
            sems.at[index],
        )
        for index in range(2)
    ]
    copies.append(
        pltpu.make_async_copy(
            field_ref.at[pl.ds(half_of(0) * HALF_PAIRS, HALF_PAIRS)], own_ref, sems.at[2]
        )
    )
    for copy in copies:
        copy.start()
    forward_tables(weight_ref, rows_ref)
    for index in range(2):
        copies[index].wait()
        span = slice(index * chunk, (index + 1) * chunk)
        forward_columns(tile_ref, span, weight_ref, high_ref, low_ref)
    forward_rows(rows_ref, high_ref, low_ref, out_ref)
    copies[2].wait()


def forward_own_kernel(tile_ref, scalar_ref, out_ref, *rest):
    *tables, weight_ref, rows_ref, high_ref, low_ref = rest
    forward_tables(weight_ref, rows_ref)
    forward_columns(tile_ref, slice(0, HALF_PAIRS), weight_ref, high_ref, low_ref)
    inverse_tables(scalar_ref, *tables)
    forward_rows(rows_ref, high_ref, low_ref, out_ref)


def forward(side, field, scalars=None):
    tile = (HALF_PAIRS, 2, ROWS, COLS)
    out_shape = [pltpu.VMEM((HALF_PAIRS, MODES, 128), F32)]
    scratch = [
        pltpu.VMEM((2 * COLS, 128), BF16),
        pltpu.VMEM((MODES, 3 * ROWS), BF16),
        pltpu.VMEM((HALF_PAIRS, ROWS, 128), BF16),
        pltpu.VMEM((HALF_PAIRS, ROWS, 128), BF16),
    ]
    if side == 0:
        out_shape += [
            jax.ShapeDtypeStruct((ROWS, 3 * MODES), BF16),
            jax.ShapeDtypeStruct((ROWS, 3 * MODES), BF16),
            jax.ShapeDtypeStruct((4 * MODES, COLS), BF16),
            jax.ShapeDtypeStruct((4 * MODES, COLS), BF16),
            jax.ShapeDtypeStruct((6 * MODES, 256), BF16),
            jax.ShapeDtypeStruct((PAIRS, 128), F32),
        ]
    else:
        out_shape.append(pltpu.VMEM(tile, BF16))
        scratch = [pltpu.VMEM(tile, BF16), *scratch, pltpu.SemaphoreType.DMA((3,))]
    return pl.pallas_call(
        forward_own_kernel if side == 0 else forward_other_kernel,
        in_specs=[VMEM, SMEM] if side == 0 else [ANY],
        out_specs=[VMEM] * len(out_shape),
        out_shape=out_shape,
        scratch_shapes=scratch,
        compiler_params=pltpu.CompilerParams(vmem_limit_bytes=VMEM_LIMIT),
        cost_estimate=pl.CostEstimate(
            flops=2 * HALF_PAIRS * 2 * ROWS * COLS * MODES,
            bytes_accessed=HALF_PAIRS * 2 * ROWS * COLS * 2 + HALF_PAIRS * MODES * 128 * 4,
            transcendentals=0,
        ),
        name="forward_own" if side == 0 else "forward_other",
    )(*([field, scalars] if side == 0 else [field]))


def turning_table(shift_x):
    shape = (128, 256)
    source, target = row_index(shape), lane_mode(shape)
    source_mode, mode = source & (MODES - 1), target & (MODES - 1)
    same = (source >= MODES) == ((target & 127) >= MODES)
    highest = target >= 128
    wave = jnp.where(highest, HALF, wave_number(mode))
    cosine = wave_sine(wave * shift_x + CELLS // 4)
    sine = wave_sine(wave * shift_x)
    to_cosine = (mode < HALF) & (source_mode == mode + (HALF - 1))
    to_sine = (mode >= HALF) & (source_mode == mode - (HALF - 1)) & (mode != MODES - 1)
    turned = jnp.where(to_cosine, sine, jnp.where(to_sine, -sine, 0.0))
    turned = jnp.where(source_mode == mode, cosine, turned)
    turned = jnp.where(same, turned, 0.0)
    last = jnp.where((source_mode == MODES - 1) & (mode < 3) & jnp.logical_not(same), sine, 0.0)
    return jnp.where(highest, last, turned)


def inverse_tables(
    scalar_ref, rows_ref, parent_rows_ref, even_ref, odd_ref, turning_ref, gain_ref
):
    first_x = lax.axis_index("gx") * COLS
    first_y = lax.axis_index("gy") * ROWS
    shift_x = scalar_ref[0].astype(jnp.int32)
    shift_y = scalar_ref[1].astype(jnp.int32)
    shape = (ROWS, 128)
    lane = lane_mode(shape)
    mode = lane & (MODES - 1)
    position = row_index(shape) + first_y + jnp.where(lane < MODES, 0, shift_y)
    value = wave_value(mode, position)
    value = jnp.where((lane >= MODES) | (mode == 0), value, 2.0 * value)
    high, low = split_bf16(value)
    nest, parent = slice(0, MODES), slice(MODES, 128)
    rows_ref[...] = jnp.concatenate([high[:, nest], high[:, nest], low[:, nest]], axis=1)
    parent_rows_ref[...] = jnp.concatenate(
        [high[:, parent], high[:, parent], low[:, parent]], axis=1
    )
    shape = (MODES, COLS)
    position = lane_mode(shape) + first_x
    high, low = split_bf16(wave_value(row_index(shape), position))
    highest = wave_sine(HALF * position + CELLS // 4)
    highest_high, highest_low = split_bf16(highest)
    row = row_index(shape)
    zero = jnp.zeros(shape, BF16)
    extra = jnp.where(row < 2, highest_high, jnp.where(row == 2, highest_low, zero))
    even_ref[...] = jnp.concatenate([high, high, low, extra], axis=0)
    odd_ref[...] = jnp.concatenate([high, high, extra, low], axis=0)
    high, low = split_bf16(turning_table(shift_x))
    turning_ref[...] = jnp.concatenate([high, high, low], axis=0)
    left = lane_mode((1, 128)) < MODES
    for pair in range(PAIRS):
        field, level = divmod(2 * pair, LEVELS)
        strength = scalar_ref[18 + field]
        gain_ref[pair : pair + 1, :] = jnp.where(
            left, strength * scalar_ref[2 + level], strength * scalar_ref[3 + level]
        )


def parent_kernel(
    parent_ref, after_ref, parent_rows_ref, turning_ref, gain_ref, scaled_ref, along_ref, last_ref
):
    del after_ref
    mode = lane_mode((PAIRS, 128)) & (MODES - 1)
    scaled_ref[...] = gain_ref[...] * (jnp.where(mode == 0, -1.0, -2.0) / (CELLS * CELLS))
    is_low = lane_mode((ROWS, 256)) & (MODES - 1) == 1
    for start in range(0, PAIRS, TURN):
        rows = []
        for pair in range(start, start + TURN):
            both = jnp.concatenate([parent_ref[pair, 0], parent_ref[pair, 1]], axis=1)
            high, low = split_bf16(both * gain_ref[pair : pair + 1, :])
            rows.append(jnp.concatenate([high, low, high], axis=1))
        turned = jnp.dot(
            jnp.concatenate(rows, axis=0), turning_ref[...], preferred_element_type=F32
        )
        for pair in range(0, TURN, 2):
            first = turned[pair * MODES : (pair + 1) * MODES]
            second = turned[(pair + 1) * MODES : (pair + 2) * MODES]
            high, low = split_bf16(jnp.concatenate([first[:, 0:128], second[:, 0:128]], axis=1))
            stacked = jnp.concatenate([high, low, high], axis=0)
            along = jnp.dot(parent_rows_ref[...], stacked, preferred_element_type=F32)
            high, low = split_bf16(jnp.concatenate([first[:, 128:], second[:, 128:]], axis=1))
            stacked = jnp.concatenate([high, low, high], axis=0)
            last = jnp.dot(parent_rows_ref[...], stacked, preferred_element_type=F32)
            high, low = split_bf16(last)
            last = jnp.where(is_low, low, high)
            for slot in range(2):
                lanes = slice(slot * 128, (slot + 1) * 128)
                along_ref[start + pair + slot] = along[:, lanes]
                last_ref[start + pair + slot] = last[:, lanes]


def parent_along_rows(parent, after, parent_rows, turning, gain):
    return pl.pallas_call(
        parent_kernel,
        in_specs=[VMEM, ANY, VMEM, VMEM, VMEM],
        out_specs=[VMEM] * 3,
        out_shape=[
            jax.ShapeDtypeStruct((PAIRS, 128), F32),
            jax.ShapeDtypeStruct((PAIRS, ROWS, 128), F32),
            jax.ShapeDtypeStruct((PAIRS, ROWS, 128), BF16),
        ],
        compiler_params=pltpu.CompilerParams(vmem_limit_bytes=VMEM_LIMIT),
        cost_estimate=pl.CostEstimate(
            flops=20 * PAIRS * ROWS * 128 * 3 * MODES,
            bytes_accessed=PAIRS * MODES * 128 * 8,
            transcendentals=0,
        ),
        name="parent_along_rows",
    )(parent, after, parent_rows, turning, gain)


def inverse_kernel(
    side, modes_ref, field_ref, rows_ref, even_ref, odd_ref, gain_ref, along_ref, last_ref, *rest
):
    first_pair = half_of(side) * HALF_PAIRS
    copies = []
    if side == 0:
        out_ref, held_ref, result_ref, left_ref, sems = rest
        chunks = INVERSE_OWN
    else:
        held_ref, _, out_ref, result_ref, left_ref, sems = rest
        chunks = INVERSE_OTHER
        first_held = half_of(0) * HALF_PAIRS + HALF_PAIRS - HELD
        copies.append(
            pltpu.make_async_copy(
                held_ref, out_ref.at[pl.ds(first_held, HELD)], sems.at[len(chunks)]
            )
        )
        copies[0].start()
    left = lane_mode((ROWS, 128)) < MODES
    start = 0
    for index, chunk in enumerate(chunks):
        span = slice(start, start + chunk)
        for here in range(start, start + chunk, 2):
            nest = []
            for pair in (here, here + 1):
                nest.append(modes_ref[pair] * gain_ref[pl.ds(first_pair + pair, 1), :])
            high, low = split_bf16(jnp.concatenate(nest, axis=1))
            stacked = jnp.concatenate([high, low, high], axis=0)
            nest = jnp.dot(rows_ref[...], stacked, preferred_element_type=F32)
            for slot in range(2):
                pair = here + slot
                both = nest[:, slot * 128 : (slot + 1) * 128] + along_ref[first_pair + pair]
                high = both.astype(BF16)
                low = pltpu.roll(both - high.astype(F32), MODES, 1).astype(BF16)
                last = last_ref[first_pair + pair]
                left_ref[0, pair, :, 0:128] = jnp.where(left, high, low)
                left_ref[0, pair, :, 128:256] = jnp.where(left, high, last)
                left_ref[1, pair, :, 0:128] = jnp.where(left, low, high)
                left_ref[1, pair, :, 128:256] = jnp.where(left, last, high)
        held = side == 0 and index == len(chunks) - 1
        for slot, table in enumerate((even_ref, odd_ref)):
            rows = left_ref[slot, span].reshape(chunk * ROWS, 256)
            correction = jnp.dot(rows, table[...], preferred_element_type=F32)
            correction = correction.reshape(chunk, ROWS, COLS)
            nudged = field_ref[pl.ds(first_pair + start, chunk), slot].astype(F32) + correction
            if held:
                held_ref[:, slot] = nudged.astype(BF16)
            else:
                result_ref[span, slot] = nudged.astype(BF16)
        if not held:
            copies.append(
                pltpu.make_async_copy(
                    result_ref.at[pl.ds(start, chunk)],
                    out_ref.at[pl.ds(first_pair + start, chunk)],
                    sems.at[index],
                )
            )
            copies[-1].start()
        start += chunk
    for copy in copies:
        copy.wait()


def inverse(side, modes, field, prepared, previous):
    operands = [modes, field, *prepared]
    in_specs = [VMEM] * len(operands)
    out_specs = [ANY]
    out_shape = [jax.ShapeDtypeStruct((PAIRS, 2, ROWS, COLS), BF16)]
    aliases = {}
    if side == 0:
        out_specs.append(VMEM)
        out_shape.append(pltpu.VMEM((HELD, 2, ROWS, COLS), BF16))
    else:
        out, held = previous
        operands += [held, out]
        in_specs += [VMEM, ANY]
        aliases = {len(operands) - 1: 0}
    return pl.pallas_call(
        functools.partial(inverse_kernel, side),
        in_specs=in_specs,
        out_specs=out_specs,
        out_shape=out_shape,
        scratch_shapes=[
            pltpu.VMEM((HALF_PAIRS, 2, ROWS, COLS), BF16),
            pltpu.VMEM((2, HALF_PAIRS, ROWS, 256), BF16),
            pltpu.SemaphoreType.DMA((4,)),
        ],
        input_output_aliases=aliases,
        compiler_params=pltpu.CompilerParams(vmem_limit_bytes=VMEM_LIMIT),
        cost_estimate=pl.CostEstimate(
            flops=2 * HALF_PAIRS * 2 * ROWS * COLS * 4 * MODES,
            bytes_accessed=HALF_PAIRS * 2 * ROWS * COLS * 4 + HALF_PAIRS * MODES * 128 * 4,
            transcendentals=0,
        ),
        name="inverse_own" if side == 0 else "inverse_other",
    )(*operands)


def reduce_groups():
    return [
        [(2 * y + core) * 16 + 4 * z + x for z in pair for y in range(4) for x in range(4)]
        for core in range(2)
        for pair in ((0, 1), (3, 2))
    ]


CORE_SWAP = [(i, i ^ 1) for i in range(8)]
Z_SWAP = [(4 * z + x, 4 * (3 - z) + x) for z in range(4) for x in range(4)]


def sum_kernel(pieces_ref, out_ref):
    out_ref[...] = jnp.sum(pieces_ref[...], axis=0)


def sum_pieces(pieces):
    return pl.pallas_call(
        sum_kernel,
        in_specs=[VMEM],
        out_specs=VMEM,
        out_shape=pltpu.VMEM(pieces.shape[1:], F32),
        compiler_params=pltpu.CompilerParams(vmem_limit_bytes=VMEM_LIMIT),
        name="sum_pieces",
    )(pltpu.with_memory_space_constraint(pieces, pltpu.VMEM))


def per_device(nest_fields, parent_modes, nest_offset, level_mask, strength):
    field = nest_fields.reshape(PAIRS, 2, ROWS, COLS)
    field = pltpu.with_memory_space_constraint(field, pltpu.HBM)
    parent = parent_modes.reshape(PAIRS, 2, MODES, MODES)
    scalars = jnp.concatenate([nest_offset.astype(F32), level_mask.astype(F32), strength])
    groups = reduce_groups()
    members = len(groups[0])

    for_partner, own_tile = forward(1, field)
    from_partner = lax.ppermute(for_partner, "gx", CORE_SWAP)
    own, rows, parent_rows, even, odd, turning, gain = forward(0, own_tile, scalars)
    own = (own + from_partner).reshape(members, -1, 128)

    def exchange(pieces):
        return lax.all_to_all(pieces, ("gx", "gy"), 0, 0, axis_index_groups=groups, tiled=True)

    piece = sum_pieces(exchange(own))
    from_pair = lax.ppermute(piece, "gy", Z_SWAP)
    parents = parent_along_rows(parent, piece, parent_rows, turning, gain)
    from_pair, parents = lax.optimization_barrier((from_pair, parents))
    prepared = [rows, even, odd, *parents]
    piece = piece + from_pair
    sums = exchange(jnp.broadcast_to(piece[None], (members,) + piece.shape))
    sums = sums.reshape(HALF_PAIRS, MODES, 128)
    other_sums = lax.ppermute(sums, "gx", CORE_SWAP)
    whole = nest_fields.reshape(PAIRS, 2, ROWS, COLS)
    previous = inverse(0, sums, whole, prepared, None)
    (out,) = inverse(1, other_sums, whole, prepared, previous)
    return out.reshape(nest_fields.shape)


def solution(mesh):
    in_specs = (P(None, None, "gy", "gx"), P(), P(), P(), P())
    out_specs = P(None, None, "gy", "gx")
    return jax.shard_map(
        per_device, mesh=mesh, in_specs=in_specs, out_specs=out_specs, check_vma=False
    )
```

```python
import functools
import math

import jax
import jax.numpy as jnp
from jax import lax
from jax.experimental import pallas as pl
from jax.experimental.pallas import tpu as pltpu
from jax.sharding import PartitionSpec as P

MODES = 64
HALF = MODES // 2
CELLS = 2048
ROWS = 128
COLS = 256
SLABS = 80
LEVELS = 16
PAIRS = SLABS // 2
HALF_PAIRS = PAIRS // 2
INVERSE_OWN = (6, 8, 6)
INVERSE_OTHER = (10, 6, 4)
HELD = INVERSE_OWN[-1]
TURN = 8
F32 = jnp.float32
BF16 = jnp.bfloat16
VMEM_LIMIT = 16 * 1024 * 1024
VMEM = pl.BlockSpec(memory_space=pltpu.VMEM)
SMEM = pl.BlockSpec(memory_space=pltpu.SMEM)
ANY = pl.BlockSpec(memory_space=pl.ANY)


def split_bf16(value):
    high = value.astype(BF16)
    low = (value - high.astype(F32)).astype(BF16)
    return high, low


def wave_number(mode):
    return jnp.where(mode < HALF, mode, mode - (HALF - 1))


def wave_value(mode, position):
    return wave_sine(wave_number(mode) * position + jnp.where(mode < HALF, CELLS // 4, 0))


def wave_sine(phase):
    phase = ((phase + CELLS // 2) & (CELLS - 1)) - CELLS // 2
    size = jnp.abs(phase)
    size = jnp.minimum(size, CELLS // 2 - size)
    angle = jnp.where(phase < 0, -size, size).astype(F32) * (2.0 * math.pi / CELLS)
    square = angle * angle
    total = jnp.full_like(square, 1.0 / math.factorial(13))
    for degree in (11, 9, 7, 5, 3, 1):
        sign = -1.0 if degree % 4 == 3 else 1.0
        total = total * square + sign / math.factorial(degree)
    return angle * total


def lane_mode(shape):
    return lax.broadcasted_iota(jnp.int32, shape, 1)


def row_index(shape):
    return lax.broadcasted_iota(jnp.int32, shape, 0)


def half_of(side):
    core = lax.axis_index("gx") & 1
    return core if side == 0 else 1 - core


def forward_tables(weight_ref, rows_ref):
    lane = lane_mode((COLS, 128))
    first_x = lax.axis_index("gx") * COLS
    table = wave_value(lane & (MODES - 1), row_index((COLS, 128)) + first_x)
    weight_ref[0:COLS, :] = jnp.where(lane < MODES, table, 0.0).astype(BF16)
    weight_ref[COLS:, :] = jnp.where(lane < MODES, 0.0, table).astype(BF16)
    first_y = lax.axis_index("gy") * ROWS
    shape = (MODES, ROWS)
    high, low = split_bf16(wave_value(row_index(shape), lane_mode(shape) + first_y))
    rows_ref[...] = jnp.concatenate([high, high, low], axis=1)


def forward_columns(tile_ref, span, weight_ref, high_ref, low_ref):
    pairs = span.stop - span.start
    left = tile_ref[span, 0].reshape(pairs * ROWS, COLS)
    right = tile_ref[span, 1].reshape(pairs * ROWS, COLS)
    along = jnp.dot(
        jnp.concatenate([left, right], axis=1), weight_ref[...], preferred_element_type=F32
    )
    high, low = split_bf16(along)
    high_ref[span] = high.reshape(pairs, ROWS, 128)
    low_ref[span] = low.reshape(pairs, ROWS, 128)


def forward_rows(rows_ref, high_ref, low_ref, out_ref):
    for pair in range(0, HALF_PAIRS, 2):
        high = jnp.concatenate([high_ref[pair], high_ref[pair + 1]], axis=1)
        low = jnp.concatenate([low_ref[pair], low_ref[pair + 1]], axis=1)
        stacked = jnp.concatenate([high, low, high], axis=0)
        sums = jnp.dot(rows_ref[...], stacked, preferred_element_type=F32)
        out_ref[pair] = sums[:, 0:128]
        out_ref[pair + 1] = sums[:, 128:256]


def forward_other_kernel(
    field_ref, out_ref, own_ref, tile_ref, weight_ref, rows_ref, high_ref, low_ref, sems
):
    first_pair = half_of(1) * HALF_PAIRS
    chunk = HALF_PAIRS // 2
    copies = [
        pltpu.make_async_copy(
            field_ref.at[pl.ds(first_pair + index * chunk, chunk)],
            tile_ref.at[pl.ds(index * chunk, chunk)],
            sems.at[index],
        )
        for index in range(2)
    ]
    copies.append(
        pltpu.make_async_copy(
            field_ref.at[pl.ds(half_of(0) * HALF_PAIRS, HALF_PAIRS)], own_ref, sems.at[2]
        )
    )
    for copy in copies:
        copy.start()
    forward_tables(weight_ref, rows_ref)
    for index in range(2):
        copies[index].wait()
        span = slice(index * chunk, (index + 1) * chunk)
        forward_columns(tile_ref, span, weight_ref, high_ref, low_ref)
    forward_rows(rows_ref, high_ref, low_ref, out_ref)
    copies[2].wait()


def forward_own_kernel(tile_ref, scalar_ref, out_ref, *rest):
    *tables, weight_ref, rows_ref, high_ref, low_ref = rest
    forward_tables(weight_ref, rows_ref)
    forward_columns(tile_ref, slice(0, HALF_PAIRS), weight_ref, high_ref, low_ref)
    inverse_tables(scalar_ref, *tables)
    forward_rows(rows_ref, high_ref, low_ref, out_ref)


def forward(side, field, scalars=None):
    tile = (HALF_PAIRS, 2, ROWS, COLS)
    out_shape = [pltpu.VMEM((HALF_PAIRS, MODES, 128), F32)]
    scratch = [
        pltpu.VMEM((2 * COLS, 128), BF16),
        pltpu.VMEM((MODES, 3 * ROWS), BF16),
        pltpu.VMEM((HALF_PAIRS, ROWS, 128), BF16),
        pltpu.VMEM((HALF_PAIRS, ROWS, 128), BF16),
    ]
    if side == 0:
        out_shape += [
            jax.ShapeDtypeStruct((ROWS, 3 * MODES), BF16),
            jax.ShapeDtypeStruct((ROWS, 3 * MODES), BF16),
            jax.ShapeDtypeStruct((4 * MODES, COLS), BF16),
            jax.ShapeDtypeStruct((4 * MODES, COLS), BF16),
            jax.ShapeDtypeStruct((6 * MODES, 256), BF16),
            jax.ShapeDtypeStruct((PAIRS, 128), F32),
        ]
    else:
        out_shape.append(pltpu.VMEM(tile, BF16))
        scratch = [pltpu.VMEM(tile, BF16), *scratch, pltpu.SemaphoreType.DMA((3,))]
    return pl.pallas_call(
        forward_own_kernel if side == 0 else forward_other_kernel,
        in_specs=[VMEM, SMEM] if side == 0 else [ANY],
        out_specs=[VMEM] * len(out_shape),
        out_shape=out_shape,
        scratch_shapes=scratch,
        compiler_params=pltpu.CompilerParams(vmem_limit_bytes=VMEM_LIMIT),
        cost_estimate=pl.CostEstimate(
            flops=2 * HALF_PAIRS * 2 * ROWS * COLS * MODES,
            bytes_accessed=HALF_PAIRS * 2 * ROWS * COLS * 2 + HALF_PAIRS * MODES * 128 * 4,
            transcendentals=0,
        ),
        name="forward_own" if side == 0 else "forward_other",
    )(*([field, scalars] if side == 0 else [field]))


def turning_table(shift_x):
    shape = (128, 256)
    source, target = row_index(shape), lane_mode(shape)
    source_mode, mode = source & (MODES - 1), target & (MODES - 1)
    same = (source >= MODES) == ((target & 127) >= MODES)
    highest = target >= 128
    wave = jnp.where(highest, HALF, wave_number(mode))
    cosine = wave_sine(wave * shift_x + CELLS // 4)
    sine = wave_sine(wave * shift_x)
    to_cosine = (mode < HALF) & (source_mode == mode + (HALF - 1))
    to_sine = (mode >= HALF) & (source_mode == mode - (HALF - 1)) & (mode != MODES - 1)
    turned = jnp.where(to_cosine, sine, jnp.where(to_sine, -sine, 0.0))
    turned = jnp.where(source_mode == mode, cosine, turned)
    turned = jnp.where(same, turned, 0.0)
    last = jnp.where((source_mode == MODES - 1) & (mode < 3) & jnp.logical_not(same), sine, 0.0)
    return jnp.where(highest, last, turned)


def inverse_tables(
    scalar_ref, rows_ref, parent_rows_ref, even_ref, odd_ref, turning_ref, gain_ref
):
    first_x = lax.axis_index("gx") * COLS
    first_y = lax.axis_index("gy") * ROWS
    shift_x = scalar_ref[0].astype(jnp.int32)
    shift_y = scalar_ref[1].astype(jnp.int32)
    shape = (ROWS, 128)
    lane = lane_mode(shape)
    mode = lane & (MODES - 1)
    position = row_index(shape) + first_y + jnp.where(lane < MODES, 0, shift_y)
    value = wave_value(mode, position)
    value = jnp.where((lane >= MODES) | (mode == 0), value, 2.0 * value)
    high, low = split_bf16(value)
    nest, parent = slice(0, MODES), slice(MODES, 128)
    rows_ref[...] = jnp.concatenate([high[:, nest], high[:, nest], low[:, nest]], axis=1)
    parent_rows_ref[...] = jnp.concatenate(
        [high[:, parent], high[:, parent], low[:, parent]], axis=1
    )
    shape = (MODES, COLS)
    position = lane_mode(shape) + first_x
    high, low = split_bf16(wave_value(row_index(shape), position))
    highest = wave_sine(HALF * position + CELLS // 4)
    highest_high, highest_low = split_bf16(highest)
    row = row_index(shape)
    zero = jnp.zeros(shape, BF16)
    extra = jnp.where(row < 2, highest_high, jnp.where(row == 2, highest_low, zero))
    even_ref[...] = jnp.concatenate([high, high, low, extra], axis=0)
    odd_ref[...] = jnp.concatenate([high, high, extra, low], axis=0)
    high, low = split_bf16(turning_table(shift_x))
    turning_ref[...] = jnp.concatenate([high, high, low], axis=0)
    left = lane_mode((1, 128)) < MODES
    for pair in range(PAIRS):
        field, level = divmod(2 * pair, LEVELS)
        strength = scalar_ref[18 + field]
        gain_ref[pair : pair + 1, :] = jnp.where(
            left, strength * scalar_ref[2 + level], strength * scalar_ref[3 + level]
        )


def parent_kernel(
    parent_ref, after_ref, parent_rows_ref, turning_ref, gain_ref, scaled_ref, along_ref, last_ref
):
    del after_ref
    mode = lane_mode((PAIRS, 128)) & (MODES - 1)
    scaled_ref[...] = gain_ref[...] * (jnp.where(mode == 0, -1.0, -2.0) / (CELLS * CELLS))
    is_low = lane_mode((ROWS, 256)) & (MODES - 1) == 1
    for start in range(0, PAIRS, TURN):
        rows = []
        for pair in range(start, start + TURN):
            both = jnp.concatenate([parent_ref[pair, 0], parent_ref[pair, 1]], axis=1)
            high, low = split_bf16(both * gain_ref[pair : pair + 1, :])
            rows.append(jnp.concatenate([high, low, high], axis=1))
        turned = jnp.dot(
            jnp.concatenate(rows, axis=0), turning_ref[...], preferred_element_type=F32
        )
        for pair in range(0, TURN, 2):
            first = turned[pair * MODES : (pair + 1) * MODES]
            second = turned[(pair + 1) * MODES : (pair + 2) * MODES]
            high, low = split_bf16(jnp.concatenate([first[:, 0:128], second[:, 0:128]], axis=1))
            stacked = jnp.concatenate([high, low, high], axis=0)
            along = jnp.dot(parent_rows_ref[...], stacked, preferred_element_type=F32)
            high, low = split_bf16(jnp.concatenate([first[:, 128:], second[:, 128:]], axis=1))
            stacked = jnp.concatenate([high, low, high], axis=0)
            last = jnp.dot(parent_rows_ref[...], stacked, preferred_element_type=F32)
            high, low = split_bf16(last)
            last = jnp.where(is_low, low, high)
            for slot in range(2):
                lanes = slice(slot * 128, (slot + 1) * 128)
                along_ref[start + pair + slot] = along[:, lanes]
                last_ref[start + pair + slot] = last[:, lanes]


def parent_along_rows(parent, after, parent_rows, turning, gain):
    return pl.pallas_call(
        parent_kernel,
        in_specs=[VMEM, ANY, VMEM, VMEM, VMEM],
        out_specs=[VMEM] * 3,
        out_shape=[
            jax.ShapeDtypeStruct((PAIRS, 128), F32),
            jax.ShapeDtypeStruct((PAIRS, ROWS, 128), F32),
            jax.ShapeDtypeStruct((PAIRS, ROWS, 128), BF16),
        ],
        compiler_params=pltpu.CompilerParams(vmem_limit_bytes=VMEM_LIMIT),
        cost_estimate=pl.CostEstimate(
            flops=20 * PAIRS * ROWS * 128 * 3 * MODES,
            bytes_accessed=PAIRS * MODES * 128 * 8,
            transcendentals=0,
        ),
        name="parent_along_rows",
    )(parent, after, parent_rows, turning, gain)


def inverse_kernel(
    side, modes_ref, field_ref, rows_ref, even_ref, odd_ref, gain_ref, along_ref, last_ref, *rest
):
    first_pair = half_of(side) * HALF_PAIRS
    copies = []
    if side == 0:
        out_ref, held_ref, result_ref, left_ref, sems = rest
        chunks = INVERSE_OWN
    else:
        held_ref, _, out_ref, result_ref, left_ref, sems = rest
        chunks = INVERSE_OTHER
        first_held = half_of(0) * HALF_PAIRS + HALF_PAIRS - HELD
        copies.append(
            pltpu.make_async_copy(
                held_ref, out_ref.at[pl.ds(first_held, HELD)], sems.at[len(chunks)]
            )
        )
        copies[0].start()
    left = lane_mode((ROWS, 128)) < MODES
    start = 0
    for index, chunk in enumerate(chunks):
        span = slice(start, start + chunk)
        for here in range(start, start + chunk, 2):
            nest = []
            for pair in (here, here + 1):
                nest.append(modes_ref[pair] * gain_ref[pl.ds(first_pair + pair, 1), :])
            high, low = split_bf16(jnp.concatenate(nest, axis=1))
            stacked = jnp.concatenate([high, low, high], axis=0)
            nest = jnp.dot(rows_ref[...], stacked, preferred_element_type=F32)
            for slot in range(2):
                pair = here + slot
                both = nest[:, slot * 128 : (slot + 1) * 128] + along_ref[first_pair + pair]
                high = both.astype(BF16)
                low = pltpu.roll(both - high.astype(F32), MODES, 1).astype(BF16)
                last = last_ref[first_pair + pair]
                left_ref[0, pair, :, 0:128] = jnp.where(left, high, low)
                left_ref[0, pair, :, 128:256] = jnp.where(left, high, last)
                left_ref[1, pair, :, 0:128] = jnp.where(left, low, high)
                left_ref[1, pair, :, 128:256] = jnp.where(left, last, high)
        held = side == 0 and index == len(chunks) - 1
        for slot, table in enumerate((even_ref, odd_ref)):
            rows = left_ref[slot, span].reshape(chunk * ROWS, 256)
            correction = jnp.dot(rows, table[...], preferred_element_type=F32)
            correction = correction.reshape(chunk, ROWS, COLS)
            nudged = field_ref[pl.ds(first_pair + start, chunk), slot].astype(F32) + correction
            if held:
                held_ref[:, slot] = nudged.astype(BF16)
            else:
                result_ref[span, slot] = nudged.astype(BF16)
        if not held:
            copies.append(
                pltpu.make_async_copy(
                    result_ref.at[pl.ds(start, chunk)],
                    out_ref.at[pl.ds(first_pair + start, chunk)],
                    sems.at[index],
                )
            )
            copies[-1].start()
        start += chunk
    for copy in copies:
        copy.wait()


def inverse(side, modes, field, prepared, previous):
    operands = [modes, field, *prepared]
    in_specs = [VMEM] * len(operands)
    out_specs = [ANY]
    out_shape = [jax.ShapeDtypeStruct((PAIRS, 2, ROWS, COLS), BF16)]
    aliases = {}
    if side == 0:
        out_specs.append(VMEM)
        out_shape.append(pltpu.VMEM((HELD, 2, ROWS, COLS), BF16))
    else:
        out, held = previous
        operands += [held, out]
        in_specs += [VMEM, ANY]
        aliases = {len(operands) - 1: 0}
    return pl.pallas_call(
        functools.partial(inverse_kernel, side),
        in_specs=in_specs,
        out_specs=out_specs,
        out_shape=out_shape,
        scratch_shapes=[
            pltpu.VMEM((HALF_PAIRS, 2, ROWS, COLS), BF16),
            pltpu.VMEM((2, HALF_PAIRS, ROWS, 256), BF16),
            pltpu.SemaphoreType.DMA((4,)),
        ],
        input_output_aliases=aliases,
        compiler_params=pltpu.CompilerParams(vmem_limit_bytes=VMEM_LIMIT),
        cost_estimate=pl.CostEstimate(
            flops=2 * HALF_PAIRS * 2 * ROWS * COLS * 4 * MODES,
            bytes_accessed=HALF_PAIRS * 2 * ROWS * COLS * 4 + HALF_PAIRS * MODES * 128 * 4,
            transcendentals=0,
        ),
        name="inverse_own" if side == 0 else "inverse_other",
    )(*operands)


def reduce_groups():
    return [
        [(2 * y + core) * 16 + 4 * z + x for x in pair for y in range(4) for z in range(4)]
        for core in range(2)
        for pair in ((0, 1), (3, 2))
    ]


CORE_SWAP = [(i, i ^ 1) for i in range(8)]
X_SWAP = [(4 * z + x, 4 * z + 3 - x) for z in range(4) for x in range(4)]


def sum_kernel(pieces_ref, out_ref):
    out_ref[...] = jnp.sum(pieces_ref[...], axis=0)


def sum_pieces(pieces):
    return pl.pallas_call(
        sum_kernel,
        in_specs=[VMEM],
        out_specs=VMEM,
        out_shape=pltpu.VMEM(pieces.shape[1:], F32),
        compiler_params=pltpu.CompilerParams(vmem_limit_bytes=VMEM_LIMIT),
        name="sum_pieces",
    )(pltpu.with_memory_space_constraint(pieces, pltpu.VMEM))


def per_device(nest_fields, parent_modes, nest_offset, level_mask, strength):
    field = nest_fields.reshape(PAIRS, 2, ROWS, COLS)
    field = pltpu.with_memory_space_constraint(field, pltpu.HBM)
    parent = parent_modes.reshape(PAIRS, 2, MODES, MODES)
    scalars = jnp.concatenate([nest_offset.astype(F32), level_mask.astype(F32), strength])
    groups = reduce_groups()
    members = len(groups[0])

    for_partner, own_tile = forward(1, field)
    from_partner = lax.ppermute(for_partner, "gx", CORE_SWAP)
    own, rows, parent_rows, even, odd, turning, gain = forward(0, own_tile, scalars)
    own = (own + from_partner).reshape(members, -1, 128)

    def exchange(pieces):
        return lax.all_to_all(pieces, ("gx", "gy"), 0, 0, axis_index_groups=groups, tiled=True)

    piece = sum_pieces(exchange(own))
    from_pair = lax.ppermute(piece, "gy", X_SWAP)
    parents = parent_along_rows(parent, piece, parent_rows, turning, gain)
    from_pair, parents = lax.optimization_barrier((from_pair, parents))
    prepared = [rows, even, odd, *parents]
    piece = piece + from_pair
    sums = exchange(jnp.broadcast_to(piece[None], (members,) + piece.shape))
    sums = sums.reshape(HALF_PAIRS, MODES, 128)
    other_sums = lax.ppermute(sums, "gx", CORE_SWAP)
    whole = nest_fields.reshape(PAIRS, 2, ROWS, COLS)
    previous = inverse(0, sums, whole, prepared, None)
    (out,) = inverse(1, other_sums, whole, prepared, previous)
    return out.reshape(nest_fields.shape)


def solution(mesh):
    in_specs = (P(None, None, "gy", "gx"), P(), P(), P(), P())
    out_specs = P(None, None, "gy", "gx")
    return jax.shard_map(
        per_device, mesh=mesh, in_specs=in_specs, out_specs=out_specs, check_vma=False
    )
```
